32 devices in a mesh: dom: 16 (over z, y, x), band: 2 (over core).
Axes of the slice: x: 2, y: 2, z: 4, core: 2. Of those that a mesh axis runs over, the one named last changes fastest.
Arguments:
- wave: float32 [8, 64, 64, 128], P('band', 'dom'), parts along dimension 0, may hold values from -6 to 6
- potential: float32 [64, 64, 128], P('dom'), may hold values from -6 to 6
- energies: float32 [8], P('band'), parts along dimension 0, may hold values from -1 to 1
- proj_index: int32 [512, 256], P('dom'), may hold values from 0 to 32767
- proj_values: float32 [512, 8, 256], P('dom'), may hold values from -4 to 4
- slot_atom: int32 [512], P('dom'), may hold values from 0 to 384, as said below
- atom_rank: int32 [384], replicated, may hold values from 0 to 383, as said below
- d_matrix: float32 [384, 8, 8], P('dom'), may hold values from -5 to 5
- q_matrix: float32 [384, 8, 8], P('dom'), may hold values from -5 to 5
Outputs:
- residual: float32 [8, 64, 64, 128], P('band', 'dom'), parts along dimension 0
The draws below stay inside these ranges and needn't reach their ends.
There are 2 independent parts, one for each index of `band`. The reference program is written for one: setup_inputs(seed, part) draws one part's arguments, and reference() takes and returns one part's arrays. A program takes and returns all parts, laid end to end along the dimension named above; an argument that names none is the same for every part. Nothing has to cross between parts.
Inputs may be any that keep to these rules, and one draw needn't show every extreme that they name: `slot_atom`: every device holds at least 8 live slots, live slots come first among a device's slots, and in every draw some device has all 32 slots live and some has only 8. The atom of a live slot on device d has atom_rank // 24 within 2 of d, counted cyclically over the devices. `atom_rank`: A permutation of the atoms.
All inputs are finite; a program needn't handle non-finite values.
Results may differ from the reference program's by a relative error of at most 0.00007.
Values sent between devices are 32-bit elements; how exact they have to be, the bound alone decides.
A program may use at most 64 MiB of HBM per device.

```python
import jax
import jax.numpy as jnp
from jax import lax

NB = 4
CX = 4
NY = 64
NZ = 128
NPROJ = 8
PTS = 256
SLOT_DEV = 32
ATOM_DEV = 24
NX = 64
SLOTS = 512
ATOMS = 384


def owner_order(key):
    return jax.random.permutation(jax.random.fold_in(key, 11), ATOMS).astype(jnp.int32)


def draw_atom_rank(key, part):
    return owner_order(key)


def draw_slot_atom(key, part):
    devices_count = SLOTS // SLOT_DEV
    ranking = owner_order(key)
    inverse = jnp.zeros((ATOMS,), jnp.int32).at[ranking].set(jnp.arange(ATOMS, dtype=jnp.int32))
    first, second, third, fourth, fifth = jax.random.split(jax.random.fold_in(key, 7), 5)
    counts = jax.random.randint(first, (devices_count,), SLOT_DEV // 4, SLOT_DEV + 1)
    full_dev = jax.random.randint(second, (), 0, devices_count)
    low_dev = (full_dev + 1 + jax.random.randint(third, (), 0, devices_count - 1)) % devices_count
    counts = counts.at[full_dev].set(SLOT_DEV).at[low_dev].set(SLOT_DEV // 4)
    within = jnp.arange(SLOTS) % SLOT_DEV
    device = jnp.arange(SLOTS) // SLOT_DEV
    offsets = jax.random.randint(fourth, (SLOTS,), -2, 3)
    owner = (device + offsets + devices_count) % devices_count
    place = owner * ATOM_DEV + jax.random.randint(fifth, (SLOTS,), 0, ATOM_DEV)
    atoms_drawn = inverse[place]
    return jnp.where(within < counts[device], atoms_drawn, ATOMS).astype(jnp.int32)


def with_ends(entries, own_key, least, largest):
    longest = entries.shape.index(max(entries.shape))
    spots = []
    for shift in (0, 1):
        where = [jax.random.randint(jax.random.fold_in(own_key, axis), (), 0, length) for axis, length in enumerate(entries.shape)]
        where[longest] = (where[longest] + shift) % entries.shape[longest]
        spots.append(tuple(where))
    return entries.at[spots[0]].set(least).at[spots[1]].set(largest)


def levels(rng, shape, cuts, least, largest):
    factor_of = 1.0
    for position, blocks in cuts:
        heights = jax.random.uniform(jax.random.fold_in(jax.random.fold_in(rng, 6), position), (blocks,), jnp.float32, least / len(cuts), largest / len(cuts))
        factor_of = factor_of * jnp.repeat(jnp.exp(heights), shape[position] // blocks).reshape((-1,) + (1,) * (len(shape) - 1 - position))
    return factor_of


def centred(key, shape, width, bound, cuts=(), kind=jnp.bfloat16):
    factor_of = levels(key, shape, cuts, -0.22, 0.18) if cuts else 1.0
    values = jax.random.normal(key, shape, jnp.float32) * width * factor_of
    return jnp.minimum(jnp.maximum(values, -bound), bound).astype(kind)


def setup_inputs(seed: int = 0, part: int = 0) -> dict:
    key_of = jax.random.split(jax.random.key(seed), 10)
    own_keys = jax.random.split(jax.random.fold_in(key_of[9], part), 10)
    return {
        "wave": centred(own_keys[0], (NB, NX, NY, NZ), 1.0, 6.0, ((1, 16),), jnp.float32),
        "potential": centred(key_of[1], (NX, NY, NZ), 1.0, 6.0, ((0, 16),), jnp.float32),
        "energies": jnp.clip(jax.random.uniform(own_keys[2], (NB,), jnp.float32, -1.0, 1.0), -1.0, 1.0),
        "proj_index": with_ends(jax.random.randint(key_of[3], (SLOTS, PTS), 0, CX * NY * NZ), jax.random.fold_in(key_of[3], 1), 0, (CX * NY * NZ) - 1).astype(jnp.int32),
        "proj_values": centred(key_of[4], (SLOTS, NPROJ, PTS), 0.25, 4.0, ((0, 16),), jnp.float32),
        "slot_atom": draw_slot_atom(jax.random.fold_in(key_of[9], 71), part),
        "atom_rank": draw_atom_rank(jax.random.fold_in(key_of[9], 71), part),
        "d_matrix": centred(key_of[7], (ATOMS, NPROJ, NPROJ), 0.35, 5.0, ((0, 16),), jnp.float32),
        "q_matrix": centred(key_of[8], (ATOMS, NPROJ, NPROJ), 0.35, 5.0, ((0, 16),), jnp.float32),
    }


HIGH = lax.Precision.HIGHEST


def laplace(field):
    total = jnp.zeros_like(field)
    for axis in (1, 2, 3):
        total = total - 2.5 * field
        total = total + (4.0 / 3.0) * (jnp.roll(field, 1, axis) + jnp.roll(field, -1, axis))
        total = total - (1.0 / 12.0) * (jnp.roll(field, 2, axis) + jnp.roll(field, -2, axis))
    return total


def reference(wave, potential, energies, proj_index, proj_values, slot_atom, atom_rank, d_matrix, q_matrix):
    bands = wave.shape[0]
    local = -0.5 * laplace(wave) + (potential[None] - energies[:, None, None, None]) * wave
    base = (jnp.arange(SLOTS) // SLOT_DEV * (CX * NY * NZ)).astype(jnp.int32)
    gidx = (proj_index + base[:, None]).astype(jnp.int32).reshape(-1)
    flat = wave.reshape(bands, -1)
    picked = flat[:, gidx].reshape(bands, SLOTS, PTS)
    coeff = jnp.einsum("nsp,sip->sni", picked, proj_values, precision=HIGH)
    live = slot_atom < ATOMS
    pos = jnp.where(live, atom_rank[jnp.minimum(slot_atom, ATOMS - 1)], ATOMS).astype(jnp.int32)
    total = jax.ops.segment_sum(coeff.reshape(SLOTS, -1), pos, num_segments=ATOMS + 1)[:ATOMS]
    total = total.reshape(ATOMS, bands, NPROJ)
    weight = jnp.einsum("aij,anj->ani", d_matrix, total, precision=HIGH)
    weight = weight - energies[None, :, None] * jnp.einsum("aij,anj->ani", q_matrix, total, precision=HIGH)
    padded = jnp.concatenate([weight, jnp.zeros((1, bands, NPROJ), jnp.float32)], axis=0)
    slot_weight = padded[pos]
    back = jnp.einsum("sni,sip->nsp", slot_weight, proj_values, precision=HIGH).reshape(bands, -1)
    result = local.reshape(bands, -1).at[:, gidx].add(back)
    return result.reshape(wave.shape)
```

```python
import functools

import jax
import jax.numpy as jnp
from jax import lax
from jax.experimental import pallas as pl
from jax.experimental.pallas import tpu as pltpu
from jax.sharding import PartitionSpec as P

HIGH = lax.Precision.HIGHEST
MESH = pl.DeviceIdType.MESH
STEPS = (-2, -1, 1, 2)
LANES = 128


def log2(size):
    bits = size.bit_length() - 1
    assert size == 1 << bits
    return bits


def iota(shape, dim):
    return lax.broadcasted_iota(jnp.int32, shape, dim)


def ones_where(mask):
    return jnp.where(mask, 1.0, 0.0).astype(jnp.float32)


def dot(a, b):
    return jnp.dot(a, b, precision=HIGH, preferred_element_type=jnp.float32)


def dot_dims(a, b, left, right, precision=None):
    return lax.dot_general(
        a, b, (((left,), (right,)), ((), ())),
        precision=precision, preferred_element_type=jnp.float32,
    )


def halves(value):
    high = value.astype(jnp.bfloat16)
    low = (value - high.astype(jnp.float32)).astype(jnp.bfloat16)
    return high, low


def kernel(
    n_dom, unroll,
    energies, wave, potential, index, values, slot_atom, atom_rank, effective,
    out,
    low_halo, high_halo, turned, row_hot, col_hot, picked, back_rows, acc,
    parts, arrived, windows, send_sem, recv_sem,
):
    bands, planes, ny, nz = wave.shape
    slots, pts = index.shape
    nproj = values.shape[0] // slots
    atoms_dev = effective.shape[0]
    atoms_all = atom_rank.shape[1]
    rows = planes * ny
    wide = bands * nz
    row_shift, lane_mask = log2(nz), nz - 1
    p_bits, s_bits = log2(nproj), log2(slots)

    me = lax.axis_index("dom")

    def device(step):
        return lax.rem(me + step + n_dom, n_dom)

    barrier = pltpu.get_barrier_semaphore()
    for step in STEPS:
        pl.semaphore_signal(barrier, inc=1, device_id={"dom": device(step)}, device_id_type=MESH)

    for n in range(bands):
        block = wave[n].reshape(rows, nz).T
        high, low = halves(block)
        turned[n * nz : (n + 1) * nz, :rows] = high
        turned[n * nz : (n + 1) * nz, rows:] = low

    pl.semaphore_wait(barrier, len(STEPS))

    def copy(k, src, dst, step):
        return pltpu.make_async_remote_copy(
            src_ref=src, dst_ref=dst, send_sem=send_sem.at[k], recv_sem=recv_sem.at[k],
            device_id={"dom": device(step)}, device_id_type=MESH,
        )

    halo = [
        copy(0, wave.at[:, planes - 2 : planes], low_halo, 1),
        copy(1, wave.at[:, 0:2], high_halo, -1),
    ]
    for c in halo:
        c.start()

    def gather(group, carry):
        for u in range(unroll):
            s = group * unroll + u
            flat = index[pl.ds(s, 1), :]
            r = lax.shift_right_logical(flat, row_shift)
            c = flat & lane_mask
            hot = ones_where(iota((rows, pts), 0) == r).astype(jnp.bfloat16)
            row_hot[s] = hot
            match = iota((nz, pts), 0) == c
            col_hot[s] = ones_where(match).astype(jnp.bfloat16)
            lines = jnp.dot(
                turned[...], jnp.concatenate([hot, hot], axis=0),
                preferred_element_type=jnp.float32,
            )
            for n in range(bands):
                line = jnp.where(match, lines[n * nz : (n + 1) * nz], 0.0)
                picked[n, pl.ds(s, 1), :] = jnp.sum(line, axis=0, keepdims=True)
        return carry

    lax.fori_loop(0, slots // unroll, gather, 0)

    eye = iota((slots, slots), 0) == iota((slots, slots), 1)
    atom = jnp.sum(jnp.where(eye, slot_atom[...].astype(jnp.float32), 0.0), axis=1, keepdims=True)
    rank = atom_rank[...].astype(jnp.float32) + 1.0
    among = iota((slots, atoms_all), 1).astype(jnp.float32) == atom
    position = jnp.sum(jnp.where(among, rank, 0.0), axis=1, keepdims=True)
    spots = iota((slots, 5 * atoms_dev), 1)
    owned = spots
    for b in range(5):
        inside = (spots >= b * atoms_dev) & (spots < (b + 1) * atoms_dev)
        owned = owned + jnp.where(inside, (device(b - 2) - b) * atoms_dev, 0)
    table = ones_where((owned + 1).astype(jnp.float32) == position)

    ns, si = bands * slots, slots * nproj
    same_slot = (iota((ns, si), 0) & (slots - 1)) == lax.shift_right_logical(iota((ns, si), 1), p_bits)
    same_band = lax.shift_right_logical(iota((ns, LANES), 0), s_bits) == lax.shift_right_logical(
        iota((ns, LANES), 1), p_bits
    )
    spread = ones_where(
        ((iota((LANES, si), 0) & (nproj - 1)) == (iota((LANES, si), 1) & (nproj - 1)))
        & (iota((LANES, si), 0) < bands * nproj)
    )
    pairs = dot_dims(picked[...].reshape(ns, pts), values[...], 1, 1, HIGH)
    pairs = jnp.where(same_slot, pairs, 0.0)
    slot_rows = jnp.where(same_band, dot_dims(pairs, spread, 1, 1, HIGH), 0.0)
    coeff = jnp.sum(slot_rows.reshape(bands, slots, LANES), axis=0)
    partial = dot_dims(table, coeff, 0, 0, HIGH)
    parts[...] = partial.reshape(5, atoms_dev, LANES)

    first = [copy(2 + i, parts.at[step + 2], arrived.at[i], step) for i, step in enumerate(STEPS)]
    for c in first:
        c.start()

    def local(some):
        for n in some:
            for x in range(planes):
                f = wave[n, x]

                def plane(k):
                    if k < 0:
                        return low_halo[n, k + 2]
                    if k >= planes:
                        return high_halo[n, k - planes]
                    return wave[n, k]

                near = plane(x - 1) + plane(x + 1)
                far = plane(x - 2) + plane(x + 2)
                for axis, size in ((0, ny), (1, nz)):
                    near = near + pltpu.roll(f, 1, axis) + pltpu.roll(f, size - 1, axis)
                    far = far + pltpu.roll(f, 2, axis) + pltpu.roll(f, size - 2, axis)
                out[n, x] = (
                    (3.75 + potential[x] - energies[n]) * f - (2.0 / 3.0) * near + (1.0 / 24.0) * far
                )

    for c in halo:
        c.wait_recv()
    local(range(bands // 2))

    total = parts[2]
    for i, c in enumerate(first):
        c.wait_recv()
        total = total + arrived[i]

    nij = bands * nproj * nproj
    source, target = iota((LANES, nij), 0), iota((LANES, nij), 1)
    source_band = lax.shift_right_logical(source, p_bits)
    target_band = lax.shift_right_logical(target, 2 * p_bits)
    part_i = lax.shift_right_logical(target, p_bits) & (nproj - 1)
    part_j = target & (nproj - 1)
    source_i = source & (nproj - 1)
    by_j = ones_where((source_band == target_band) & (source_i == part_j))
    by_i = ones_where((source_band == target_band) & (source_i == part_i))
    windows[2] = dot_dims(dot(total, by_j) * effective[...], by_i, 1, 1, HIGH)

    second = [copy(6 + i, windows.at[2], windows.at[step + 2], -step) for i, step in enumerate(STEPS)]
    for c in second:
        c.start()
    local(range(bands // 2, bands))
    for c in second:
        c.wait_recv()

    slot_weight = dot(table, windows[...].reshape(5 * atoms_dev, LANES))
    slot_weight = jnp.where(same_band, jnp.concatenate([slot_weight] * bands, axis=0), 0.0)
    blocks = jnp.where(same_slot, dot(slot_weight, spread), 0.0)
    back_rows[...] = dot(blocks, values[...]).reshape(bands, slots, pts)

    acc[...] = jnp.zeros_like(acc)

    def scatter(group, carry):
        lefts, rights = [], []
        for u in range(unroll):
            s = group * unroll + u
            cols = col_hot[s].reshape(nz // 16, 16, pts)
            hot = row_hot[s]
            high_parts, low_parts = [], []
            for n in range(bands):
                line = jnp.broadcast_to(back_rows[n, pl.ds(s, 1), :], (16, pts))
                high, low = halves(line)
                high_parts.append((cols * high[None]).reshape(nz, pts))
                low_parts.append((cols * low[None]).reshape(nz, pts))
            lefts += [jnp.concatenate(high_parts, axis=0), jnp.concatenate(low_parts, axis=0)]
            rights += [hot, hot]
        acc[...] += dot_dims(jnp.concatenate(lefts, axis=1), jnp.concatenate(rights, axis=1), 1, 1)
        return carry

    lax.fori_loop(0, slots // unroll, scatter, 0)

    for n in range(bands):
        out[n] += acc[n * nz : (n + 1) * nz, :].T.reshape(planes, ny, nz)

    for c in halo + first + second:
        c.wait_send()


def per_device(
    wave, potential, energies, proj_index, proj_values, slot_atom, atom_rank, d_matrix, q_matrix
):
    bands, planes, ny, nz = wave.shape
    slots, pts = proj_index.shape
    nproj = proj_values.shape[1]
    atoms_dev = d_matrix.shape[0]
    rows = planes * ny
    effective = d_matrix[:, None] - energies[None, :, None, None] * q_matrix[:, None]
    effective = effective.reshape(atoms_dev, bands * nproj * nproj)
    f32, bf16 = jnp.float32, jnp.bfloat16
    vmem = pl.BlockSpec(memory_space=pltpu.VMEM)
    return pl.pallas_call(
        functools.partial(kernel, lax.axis_size("dom"), 2),
        out_shape=jax.ShapeDtypeStruct(wave.shape, f32),
        in_specs=[pl.BlockSpec(memory_space=pltpu.SMEM)] + [vmem] * 7,
        out_specs=vmem,
        scratch_shapes=[
            pltpu.VMEM((bands, 2, ny, nz), f32),
            pltpu.VMEM((bands, 2, ny, nz), f32),
            pltpu.VMEM((bands * nz, 2 * rows), bf16),
            pltpu.VMEM((slots, rows, pts), bf16),
            pltpu.VMEM((slots, nz, pts), bf16),
            pltpu.VMEM((bands, slots, pts), f32),
            pltpu.VMEM((bands, slots, pts), f32),
            pltpu.VMEM((bands * nz, rows), f32),
            pltpu.VMEM((5, atoms_dev, LANES), f32),
            pltpu.VMEM((4, atoms_dev, LANES), f32),
            pltpu.VMEM((5, atoms_dev, LANES), f32),
            pltpu.SemaphoreType.DMA((10,)),
            pltpu.SemaphoreType.DMA((10,)),
        ],
        compiler_params=pltpu.CompilerParams(
            collective_id=0, has_side_effects=True, vmem_limit_bytes=40 * 1024 * 1024
        ),
    )(
        energies, wave, potential, proj_index,
        proj_values.reshape(slots * nproj, pts),
        slot_atom.reshape(1, slots), atom_rank.reshape(1, -1), effective,
    )


def solution(mesh):
    placed = (
        P("band", "dom", None, None),
        P("dom", None, None),
        P("band"),
        P("dom", None),
        P("dom", None, None),
        P("dom"),
        P(),
        P("dom", None, None),
        P("dom", None, None),
    )
    return jax.shard_map(
        per_device,
        mesh=mesh,
        in_specs=placed,
        out_specs=P("band", "dom", None, None),
        check_vma=False,
    )
```

```python
import functools

import jax
import jax.numpy as jnp
from jax import lax
from jax.experimental import pallas as pl
from jax.experimental.pallas import tpu as pltpu
from jax.sharding import PartitionSpec as P

HIGH = lax.Precision.HIGHEST
MESH = pl.DeviceIdType.MESH
STEPS = (-2, -1, 1, 2)
LANES = 128


def log2(size):
    bits = size.bit_length() - 1
    assert size == 1 << bits
    return bits


def iota(shape, dim):
    return lax.broadcasted_iota(jnp.int32, shape, dim)


def ones_where(mask):
    return jnp.where(mask, 1.0, 0.0).astype(jnp.float32)


def dot(a, b):
    return jnp.dot(a, b, precision=HIGH, preferred_element_type=jnp.float32)


def dot_dims(a, b, left, right, precision=None):
    return lax.dot_general(
        a, b, (((left,), (right,)), ((), ())),
        precision=precision, preferred_element_type=jnp.float32,
    )


def halves(value):
    high = value.astype(jnp.bfloat16)
    low = (value - high.astype(jnp.float32)).astype(jnp.bfloat16)
    return high, low


def kernel(
    n_dom, unroll,
    energies, wave_in, potential_in, index_in, values_in, slot_atom_in, atom_rank_in, d_in, q_in,
    out,
    wave, potential, index, values, slot_atom, atom_rank, d_part, q_part, load_sem,
    low_halo, high_halo, turned, row_hot, col_hot, picked, back_rows, acc,
    parts, arrived, windows, send_sem, recv_sem,
):
    bands, planes, ny, nz = wave.shape
    slots, pts = index.shape
    nproj = values.shape[0] // slots
    atoms_dev = d_part.shape[2]
    atoms_all = atom_rank.shape[0]
    ni, ns, si = bands * nproj, bands * slots, slots * nproj
    rows = planes * ny
    wide = bands * nz
    row_shift, lane_mask = log2(nz), nz - 1
    p_bits, s_bits = log2(nproj), log2(slots)

    me = lax.axis_index("dom")

    loads = [
        pltpu.make_async_copy(src, dst, load_sem.at[k])
        for k, (src, dst) in enumerate((
            (wave_in, wave), (index_in, index), (slot_atom_in, slot_atom),
            (atom_rank_in, atom_rank), (values_in, values), (d_in, d_part), (q_in, q_part),
            (potential_in, potential),
        ))
    ]
    for c in loads:
        c.start()

    def device(step):
        return lax.rem(me + step + n_dom, n_dom)

    barrier = pltpu.get_barrier_semaphore()
    for step in STEPS:
        pl.semaphore_signal(barrier, inc=1, device_id={"dom": device(step)}, device_id_type=MESH)

    loads[0].wait()
    for n in range(bands):
        block = wave[n].reshape(rows, nz).T
        high, low = halves(block)
        turned[n * nz : (n + 1) * nz, :rows] = high
        turned[n * nz : (n + 1) * nz, rows:] = low

    eye = iota((slots, slots), 0) == iota((slots, slots), 1)
    for c in loads[1:4]:
        c.wait()
    atom = jnp.sum(jnp.where(eye, slot_atom[...].astype(jnp.float32), 0.0), axis=1, keepdims=True)
    rank = atom_rank[...].astype(jnp.float32).reshape(1, atoms_all) + 1.0
    among = iota((slots, atoms_all), 1).astype(jnp.float32) == atom
    position = jnp.sum(jnp.where(among, rank, 0.0), axis=1, keepdims=True)
    place = iota((slots, LANES), 1)
    tables = []
    for b in range(5):
        owned = (place + device(b - 2) * atoms_dev + 1).astype(jnp.float32)
        tables.append(ones_where((owned == position) & (place < atoms_dev)))
    table = jnp.concatenate(tables, axis=1)
    windows[2] = jnp.zeros_like(windows[2])
    acc[...] = jnp.zeros_like(acc)

    pl.semaphore_wait(barrier, len(STEPS))

    def copy(k, src, dst, step):
        return pltpu.make_async_remote_copy(
            src_ref=src, dst_ref=dst, send_sem=send_sem.at[k], recv_sem=recv_sem.at[k],
            device_id={"dom": device(step)}, device_id_type=MESH,
        )

    halo = [
        copy(0, wave.at[:, planes - 2 : planes], low_halo, 1),
        copy(1, wave.at[:, 0:2], high_halo, -1),
    ]
    for c in halo:
        c.start()

    def gather(group, carry):
        for u in range(unroll):
            s = group * unroll + u
            flat = index[pl.ds(s, 1), :]
            r = lax.shift_right_logical(flat, row_shift)
            c = flat & lane_mask
            hot = ones_where(iota((rows, pts), 0) == r).astype(jnp.bfloat16)
            row_hot[s] = hot
            match = iota((nz, pts), 0) == c
            col_hot[s] = ones_where(match).astype(jnp.bfloat16)
            lines = jnp.dot(
                turned[...], jnp.concatenate([hot, hot], axis=0),
                preferred_element_type=jnp.float32,
            )
            for n in range(bands):
                line = jnp.where(match, lines[n * nz : (n + 1) * nz], 0.0)
                picked[n, pl.ds(s, 1), :] = jnp.sum(line, axis=0, keepdims=True)
        return carry

    lax.fori_loop(0, slots // unroll, gather, 0)

    loads[4].wait()
    same_slot = (iota((ns, si), 0) & (slots - 1)) == lax.shift_right_logical(iota((ns, si), 1), p_bits)
    same_band = lax.shift_right_logical(iota((ns, ni), 0), s_bits) == lax.shift_right_logical(
        iota((ns, ni), 1), p_bits
    )
    spread = ones_where((iota((ni, si), 0) & (nproj - 1)) == (iota((ni, si), 1) & (nproj - 1)))
    pairs = dot_dims(picked[...].reshape(ns, pts), values[...], 1, 1, HIGH)
    pairs = jnp.where(same_slot, pairs, 0.0)
    slot_rows = jnp.where(same_band, dot_dims(pairs, spread, 1, 1, HIGH), 0.0)
    coeff = jnp.sum(slot_rows.reshape(bands, slots, ni), axis=0)
    partial = dot_dims(coeff, table, 0, 0, HIGH)
    for b in range(5):
        parts[b] = partial[:, b * LANES : (b + 1) * LANES]

    first = [copy(2 + i, parts.at[step + 2], arrived.at[i], step) for i, step in enumerate(STEPS)]
    for c in first:
        c.start()

    def local(some):
        for n in some:
            for x in range(planes):
                f = wave[n, x]

                def plane(k):
                    if k < 0:
                        return low_halo[n, k + 2]
                    if k >= planes:
                        return high_halo[n, k - planes]
                    return wave[n, k]

                near = plane(x - 1) + plane(x + 1)
                far = plane(x - 2) + plane(x + 2)
                for axis, size in ((0, ny), (1, nz)):
                    near = near + pltpu.roll(f, 1, axis) + pltpu.roll(f, size - 1, axis)
                    far = far + pltpu.roll(f, 2, axis) + pltpu.roll(f, size - 2, axis)
                out[n, x] = (
                    (3.75 + potential[x] - energies[n]) * f - (2.0 / 3.0) * near + (1.0 / 24.0) * far
                )

    loads[7].wait()
    for c in halo:
        c.wait_recv()
    local(range(bands // 2))

    total = parts[2]
    for i, c in enumerate(first):
        c.wait_recv()
        total = total + arrived[i]

    for c in loads[5:7]:
        c.wait()
    for n in range(bands):
        matrix = d_part[...] - energies[n] * q_part[...]
        column = total[n * nproj : (n + 1) * nproj, :atoms_dev]
        windows[2, n * nproj : (n + 1) * nproj, :atoms_dev] = jnp.sum(matrix * column[None], axis=1)

    second = [copy(6 + i, windows.at[2], windows.at[step + 2], -step) for i, step in enumerate(STEPS)]
    for c in second:
        c.start()
    local(range(bands // 2, bands))
    for c in second:
        c.wait_recv()

    around = jnp.concatenate([windows[b] for b in range(5)], axis=1)
    slot_weight = dot_dims(table, around, 1, 1, HIGH)
    slot_weight = jnp.where(same_band, jnp.concatenate([slot_weight] * bands, axis=0), 0.0)
    blocks = jnp.where(same_slot, dot(slot_weight, spread), 0.0)
    back_rows[...] = dot(blocks, values[...]).reshape(bands, slots, pts)

    def scatter(group, carry):
        lefts, rights = [], []
        for u in range(unroll):
            s = group * unroll + u
            cols = col_hot[s].reshape(nz // 16, 16, pts)
            hot = row_hot[s]
            high_parts, low_parts = [], []
            for n in range(bands):
                line = jnp.broadcast_to(back_rows[n, pl.ds(s, 1), :], (16, pts))
                high, low = halves(line)
                high_parts.append((cols * high[None]).reshape(nz, pts))
                low_parts.append((cols * low[None]).reshape(nz, pts))
            lefts += [jnp.concatenate(high_parts, axis=0), jnp.concatenate(low_parts, axis=0)]
            rights += [hot, hot]
        acc[...] += dot_dims(jnp.concatenate(lefts, axis=1), jnp.concatenate(rights, axis=1), 1, 1)
        return carry

    lax.fori_loop(0, slots // unroll, scatter, 0)

    for n in range(bands):
        out[n] += acc[n * nz : (n + 1) * nz, :].T.reshape(planes, ny, nz)

    for c in halo + first + second:
        c.wait_send()


def per_device(
    wave, potential, energies, proj_index, proj_values, slot_atom, atom_rank, d_matrix, q_matrix
):
    bands, planes, ny, nz = wave.shape
    slots, pts = proj_index.shape
    nproj = proj_values.shape[1]
    atoms_dev = d_matrix.shape[0]
    assert atoms_dev <= LANES
    rows = planes * ny
    f32, bf16 = jnp.float32, jnp.bfloat16
    vmem = pl.BlockSpec(memory_space=pltpu.VMEM)
    atom_block = (bands * nproj, LANES)
    return pl.pallas_call(
        functools.partial(kernel, lax.axis_size("dom"), 4),
        out_shape=jax.ShapeDtypeStruct(wave.shape, f32),
        in_specs=[pl.BlockSpec(memory_space=pltpu.SMEM)]
        + [pl.BlockSpec(memory_space=pltpu.HBM)] * 8,
        out_specs=vmem,
        scratch_shapes=[
            pltpu.VMEM(wave.shape, f32),
            pltpu.VMEM(potential.shape, f32),
            pltpu.VMEM(proj_index.shape, jnp.int32),
            pltpu.VMEM((slots * nproj, pts), f32),
            pltpu.VMEM((1, slots), jnp.int32),
            pltpu.VMEM(atom_rank.shape, jnp.int32),
            pltpu.VMEM((nproj, nproj, atoms_dev), f32),
            pltpu.VMEM((nproj, nproj, atoms_dev), f32),
            pltpu.SemaphoreType.DMA((8,)),
            pltpu.VMEM((bands, 2, ny, nz), f32),
            pltpu.VMEM((bands, 2, ny, nz), f32),
            pltpu.VMEM((bands * nz, 2 * rows), bf16),
            pltpu.VMEM((slots, rows, pts), bf16),
            pltpu.VMEM((slots, nz, pts), bf16),
            pltpu.VMEM((bands, slots, pts), f32),
            pltpu.VMEM((bands, slots, pts), f32),
            pltpu.VMEM((bands * nz, rows), f32),
            pltpu.VMEM((5,) + atom_block, f32),
            pltpu.VMEM((4,) + atom_block, f32),
            pltpu.VMEM((5,) + atom_block, f32),
            pltpu.SemaphoreType.DMA((10,)),
            pltpu.SemaphoreType.DMA((10,)),
        ],
        compiler_params=pltpu.CompilerParams(
            collective_id=0, has_side_effects=True, vmem_limit_bytes=60 * 1024 * 1024
        ),
    )(
        energies, wave, potential, proj_index,
        proj_values.reshape(slots * nproj, pts),
        slot_atom.reshape(1, slots), atom_rank,
        jnp.transpose(d_matrix, (1, 2, 0)), jnp.transpose(q_matrix, (1, 2, 0)),
    )


def solution(mesh):
    placed = (
        P("band", "dom", None, None),
        P("dom", None, None),
        P("band"),
        P("dom", None),
        P("dom", None, None),
        P("dom"),
        P(),
        P("dom", None, None),
        P("dom", None, None),
    )
    return jax.shard_map(
        per_device,
        mesh=mesh,
        in_specs=placed,
        out_specs=P("band", "dom", None, None),
        check_vma=False,
    )
```

```python
import functools

import jax
import jax.numpy as jnp
from jax import lax
from jax.experimental import pallas as pl
from jax.experimental.pallas import tpu as pltpu
from jax.sharding import PartitionSpec as P

MESH = pl.DeviceIdType.MESH
STEPS = (-2, -1, 1, 2)
LANES = 128


def log2(size):
    bits = size.bit_length() - 1
    assert size == 1 << bits
    return bits


def iota(shape, dim):
    return lax.broadcasted_iota(jnp.int32, shape, dim)


def ones_where(mask):
    return jnp.where(mask, 1.0, 0.0).astype(jnp.float32)


def dot_dims(a, b, left, right):
    return lax.dot_general(
        a, b, (((left,), (right,)), ((), ())), preferred_element_type=jnp.float32
    )


def dot_hot(a, hot, left, right):
    high, low = halves(a)
    hot = hot.astype(jnp.bfloat16)
    return dot_dims(high, hot, left, right) + dot_dims(low, hot, left, right)


def dot_full(a, b, left, right):
    (a_high, a_low), (b_high, b_low) = halves(a), halves(b)
    return (
        dot_dims(a_high, b_high, left, right)
        + dot_dims(a_high, b_low, left, right)
        + dot_dims(a_low, b_high, left, right)
    )


def halves(value):
    high = value.astype(jnp.bfloat16)
    low = (value - high.astype(jnp.float32)).astype(jnp.bfloat16)
    return high, low


def kernel(
    n_dom, unroll,
    energies, wave_in, potential_in, index_in, values_in, slot_atom_in, atom_rank_in, d_in, q_in,
    out,
    wave, potential, index, values, slot_atom, atom_rank, d_part, q_part, load_sem,
    low_halo, high_halo, row_hot, col_hot, picked, back_rows, acc,
    parts, arrived, windows, send_sem, recv_sem,
):
    bands, planes, ny, nz = wave.shape
    slots, pts = index.shape
    nproj = values.shape[0] // slots
    atoms_dev = d_part.shape[2]
    atoms_all = atom_rank.shape[0]
    ni, ns, si = bands * nproj, bands * slots, slots * nproj
    rows = planes * ny
    wide = bands * nz
    row_shift, lane_mask = log2(nz), nz - 1
    p_bits, s_bits = log2(nproj), log2(slots)

    me = lax.axis_index("dom")

    loads = [
        pltpu.make_async_copy(src, dst, load_sem.at[k])
        for k, (src, dst) in enumerate((
            (wave_in, wave), (index_in, index), (slot_atom_in, slot_atom),
            (atom_rank_in, atom_rank), (values_in, values), (d_in, d_part), (q_in, q_part),
            (potential_in, potential),
        ))
    ]
    for c in loads:
        c.start()

    def device(step):
        return lax.rem(me + step + n_dom, n_dom)

    barrier = pltpu.get_barrier_semaphore()
    for step in STEPS:
        pl.semaphore_signal(barrier, inc=1, device_id={"dom": device(step)}, device_id_type=MESH)

    eye = iota((slots, slots), 0) == iota((slots, slots), 1)
    for c in loads[1:4]:
        c.wait()
    atom = jnp.sum(jnp.where(eye, slot_atom[...].astype(jnp.float32), 0.0), axis=1, keepdims=True)
    rank = atom_rank[...].astype(jnp.float32).reshape(1, atoms_all) + 1.0
    among = iota((slots, atoms_all), 1).astype(jnp.float32) == atom
    position = jnp.sum(jnp.where(among, rank, 0.0), axis=1, keepdims=True)
    place = iota((slots, LANES), 1)
    tables = []
    for b in range(5):
        owned = (place + device(b - 2) * atoms_dev + 1).astype(jnp.float32)
        tables.append(ones_where((owned == position) & (place < atoms_dev)))
    table = jnp.concatenate(tables, axis=1)
    windows[2] = jnp.zeros_like(windows[2])
    acc[...] = jnp.zeros_like(acc)

    loads[0].wait()
    pl.semaphore_wait(barrier, len(STEPS))

    def copy(k, src, dst, step):
        return pltpu.make_async_remote_copy(
            src_ref=src, dst_ref=dst, send_sem=send_sem.at[k], recv_sem=recv_sem.at[k],
            device_id={"dom": device(step)}, device_id_type=MESH,
        )

    halo = [
        copy(0, wave.at[:, planes - 2 : planes], low_halo, 1),
        copy(1, wave.at[:, 0:2], high_halo, -1),
    ]
    for c in halo:
        c.start()

    tiles = [slice(k * LANES, (k + 1) * LANES) for k in range(pts // LANES)]
    at_row = lax.shift_right_logical(index[...], row_shift)
    at_col = index[...] & lane_mask
    row_tiles = [at_row[:, t] for t in tiles]
    col_tiles = [at_col[:, t] for t in tiles]

    for pair in range(0, bands, 2):
        pair_bands = range(pair, min(pair + 2, bands))

        def gather(group, found):
            x, y = group // (ny // 8), lax.rem(group, ny // 8) * 8
            blocks = [wave[n, x, pl.ds(pl.multiple_of(y, 8), 8), :] for n in pair_bands]
            found = list(found)
            for u in range(8):
                here = [r == group * 8 + u for r in row_tiles]
                k = 0
                for block in blocks:
                    row = jnp.broadcast_to(block[u : u + 1], (slots, LANES))
                    for match, c in zip(here, col_tiles):
                        line = jnp.take_along_axis(row, c, axis=1, mode="promise_in_bounds")
                        found[k] = jnp.where(match, line, found[k])
                        k += 1
            return tuple(found)

        zero = jnp.zeros((slots, LANES), jnp.float32)
        found = lax.fori_loop(0, rows // 8, gather, (zero,) * (len(pair_bands) * len(tiles)))
        for k, line in enumerate(found):
            picked[pair + k // len(tiles), :, tiles[k % len(tiles)]] = line

    loads[4].wait()
    same_slot = (iota((ns, si), 0) & (slots - 1)) == lax.shift_right_logical(iota((ns, si), 1), p_bits)
    same_band = lax.shift_right_logical(iota((ns, ni), 0), s_bits) == lax.shift_right_logical(
        iota((ns, ni), 1), p_bits
    )
    spread = ones_where((iota((ni, si), 0) & (nproj - 1)) == (iota((ni, si), 1) & (nproj - 1)))
    pairs = dot_full(picked[...].reshape(ns, pts), values[...], 1, 1)
    pairs = jnp.where(same_slot, pairs, 0.0)
    slot_rows = jnp.where(same_band, dot_hot(pairs, spread, 1, 1), 0.0)
    coeff = jnp.sum(slot_rows.reshape(bands, slots, ni), axis=0)
    partial = dot_hot(coeff.T, table, 1, 0)
    for b in range(5):
        parts[b] = partial[:, b * LANES : (b + 1) * LANES]

    first = [copy(2 + i, parts.at[step + 2], arrived.at[i], step) for i, step in enumerate(STEPS)]
    for c in first:
        c.start()

    def local(some):
        for n in some:
            for x in range(planes):
                f = wave[n, x]

                def plane(k):
                    if k < 0:
                        return low_halo[n, k + 2]
                    if k >= planes:
                        return high_halo[n, k - planes]
                    return wave[n, k]

                near = plane(x - 1) + plane(x + 1)
                far = plane(x - 2) + plane(x + 2)
                for axis, size in ((0, ny), (1, nz)):
                    near = near + pltpu.roll(f, 1, axis) + pltpu.roll(f, size - 1, axis)
                    far = far + pltpu.roll(f, 2, axis) + pltpu.roll(f, size - 2, axis)
                out[n, x] = (
                    (3.75 + potential[x] - energies[n]) * f - (2.0 / 3.0) * near + (1.0 / 24.0) * far
                )

    def hots(s, carry):
        flat = index[pl.ds(s, 1), :]
        row_hot[s] = ones_where(
            iota((rows, pts), 0) == lax.shift_right_logical(flat, row_shift)
        ).astype(jnp.bfloat16)
        col_hot[s] = ones_where(iota((nz, pts), 0) == (flat & lane_mask)).astype(jnp.bfloat16)
        return carry

    lax.fori_loop(0, slots // 2, hots, 0)
    loads[7].wait()
    for c in halo:
        c.wait_recv()
    local(range(bands // 2))

    total = parts[2]
    for i, c in enumerate(first):
        c.wait_recv()
        total = total + arrived[i]

    for c in loads[5:7]:
        c.wait()
    for n in range(bands):
        matrix = d_part[...] - energies[n] * q_part[...]
        column = total[n * nproj : (n + 1) * nproj, :atoms_dev]
        windows[2, n * nproj : (n + 1) * nproj, :atoms_dev] = jnp.sum(matrix * column[None], axis=1)

    second = [copy(6 + i, windows.at[2], windows.at[step + 2], -step) for i, step in enumerate(STEPS)]
    for c in second:
        c.start()
    lax.fori_loop(slots // 2, slots, hots, 0)
    local(range(bands // 2, bands))
    for c in second:
        c.wait_recv()

    around = jnp.concatenate([windows[b] for b in range(5)], axis=1)
    slot_weight = dot_hot(around, table, 1, 1).T
    slot_weight = jnp.where(same_band, jnp.concatenate([slot_weight] * bands, axis=0), 0.0)
    blocks = jnp.where(same_slot, dot_hot(slot_weight, spread, 1, 0), 0.0)
    back_rows[...] = dot_full(blocks, values[...], 1, 0).reshape(bands, slots, pts)

    def scatter(group, carry):
        lefts, rights = [], []
        for u in range(unroll):
            s = group * unroll + u
            cols = col_hot[s].reshape(nz // 16, 16, pts)
            high_parts, low_parts = [], []
            for n in range(bands):
                line = jnp.broadcast_to(back_rows[n, pl.ds(s, 1), :], (16, pts))
                high, low = halves(line)
                high_parts.append((cols * high[None]).reshape(nz, pts))
                low_parts.append((cols * low[None]).reshape(nz, pts))
            lefts.append(jnp.concatenate(high_parts + low_parts, axis=0))
            rights.append(row_hot[s])
        acc[...] += dot_dims(jnp.concatenate(lefts, axis=1), jnp.concatenate(rights, axis=1), 1, 1)
        return carry

    lax.fori_loop(0, slots // unroll, scatter, 0)

    for n in range(bands):
        added = acc[n * nz : (n + 1) * nz, :] + acc[wide + n * nz : wide + (n + 1) * nz, :]
        out[n] += added.T.reshape(planes, ny, nz)

    for c in halo + first + second:
        c.wait_send()


def per_device(
    wave, potential, energies, proj_index, proj_values, slot_atom, atom_rank, d_matrix, q_matrix
):
    bands, planes, ny, nz = wave.shape
    slots, pts = proj_index.shape
    nproj = proj_values.shape[1]
    atoms_dev = d_matrix.shape[0]
    assert atoms_dev <= LANES and nz == LANES
    rows = planes * ny
    f32, bf16 = jnp.float32, jnp.bfloat16
    vmem = pl.BlockSpec(memory_space=pltpu.VMEM)
    atom_block = (bands * nproj, LANES)
    return pl.pallas_call(
        functools.partial(kernel, lax.axis_size("dom"), 4),
        out_shape=jax.ShapeDtypeStruct(wave.shape, f32),
        in_specs=[pl.BlockSpec(memory_space=pltpu.SMEM)]
        + [pl.BlockSpec(memory_space=pltpu.HBM)] * 8,
        out_specs=vmem,
        scratch_shapes=[
            pltpu.VMEM(wave.shape, f32),
            pltpu.VMEM(potential.shape, f32),
            pltpu.VMEM(proj_index.shape, jnp.int32),
            pltpu.VMEM((slots * nproj, pts), f32),
            pltpu.VMEM((1, slots), jnp.int32),
            pltpu.VMEM(atom_rank.shape, jnp.int32),
            pltpu.VMEM((nproj, nproj, atoms_dev), f32),
            pltpu.VMEM((nproj, nproj, atoms_dev), f32),
            pltpu.SemaphoreType.DMA((8,)),
            pltpu.VMEM((bands, 2, ny, nz), f32),
            pltpu.VMEM((bands, 2, ny, nz), f32),
            pltpu.VMEM((slots, rows, pts), bf16),
            pltpu.VMEM((slots, nz, pts), bf16),
            pltpu.VMEM((bands, slots, pts), f32),
            pltpu.VMEM((bands, slots, pts), f32),
            pltpu.VMEM((2 * bands * nz, rows), f32),
            pltpu.VMEM((5,) + atom_block, f32),
            pltpu.VMEM((4,) + atom_block, f32),
            pltpu.VMEM((5,) + atom_block, f32),
            pltpu.SemaphoreType.DMA((10,)),
            pltpu.SemaphoreType.DMA((10,)),
        ],
        compiler_params=pltpu.CompilerParams(
            collective_id=0, has_side_effects=True, vmem_limit_bytes=60 * 1024 * 1024
        ),
    )(
        energies, wave, potential, proj_index,
        proj_values.reshape(slots * nproj, pts),
        slot_atom.reshape(1, slots), atom_rank,
        jnp.transpose(d_matrix, (1, 2, 0)), jnp.transpose(q_matrix, (1, 2, 0)),
    )


def solution(mesh):
    placed = (
        P("band", "dom", None, None),
        P("dom", None, None),
        P("band"),
        P("dom", None),
        P("dom", None, None),
        P("dom"),
        P(),
        P("dom", None, None),
        P("dom", None, None),
    )
    return jax.shard_map(
        per_device,
        mesh=mesh,
        in_specs=placed,
        out_specs=P("band", "dom", None, None),
        check_vma=False,
    )
```

```python
import functools

import jax
import jax.numpy as jnp
from jax import lax
from jax.experimental import pallas as pl
from jax.experimental.pallas import tpu as pltpu
from jax.sharding import PartitionSpec as P

MESH = pl.DeviceIdType.MESH
STEPS = (-2, -1, 1, 2)
LANES = 128


def log2(size):
    bits = size.bit_length() - 1
    assert size == 1 << bits
    return bits


def iota(shape, dim):
    return lax.broadcasted_iota(jnp.int32, shape, dim)


def ones_where(mask):
    return jnp.where(mask, 1.0, 0.0).astype(jnp.float32)


def dot_dims(a, b, left, right):
    return lax.dot_general(
        a, b, (((left,), (right,)), ((), ())), preferred_element_type=jnp.float32
    )


def dot_hot(a, hot, left, right):
    high, low = halves(a)
    hot = hot.astype(jnp.bfloat16)
    return dot_dims(high, hot, left, right) + dot_dims(low, hot, left, right)


def dot_full(a, b, left, right):
    (a_high, a_low), (b_high, b_low) = halves(a), halves(b)
    return (
        dot_dims(a_high, b_high, left, right)
        + dot_dims(a_high, b_low, left, right)
        + dot_dims(a_low, b_high, left, right)
    )


def halves(value):
    high = value.astype(jnp.bfloat16)
    low = (value - high.astype(jnp.float32)).astype(jnp.bfloat16)
    return high, low


def kernel(
    n_dom, unroll,
    energies, wave_in, potential_in, index_in, values_in, slot_atom_in, atom_rank_in, d_in, q_in,
    out,
    wave, potential, index, values, slot_atom, atom_rank, d_part, q_part, load_sem,
    low_halo, high_halo, turned, row_hot, col_hot, picked, back_rows, acc,
    parts, arrived, windows, send_sem, recv_sem,
):
    bands, planes, ny, nz = wave.shape
    slots, pts = index.shape
    nproj = values.shape[0] // slots
    atoms_dev = d_part.shape[2]
    atoms_all = atom_rank.shape[0]
    ni, ns, si = bands * nproj, bands * slots, slots * nproj
    rows = planes * ny
    wide = bands * nz
    row_shift, lane_mask = log2(nz), nz - 1
    p_bits, s_bits = log2(nproj), log2(slots)

    me = lax.axis_index("dom")

    loads = [
        pltpu.make_async_copy(src, dst, load_sem.at[k])
        for k, (src, dst) in enumerate((
            (wave_in, wave), (index_in, index), (slot_atom_in, slot_atom),
            (atom_rank_in, atom_rank), (values_in, values), (d_in, d_part), (q_in, q_part),
            (potential_in, potential),
        ))
    ]
    for c in loads:
        c.start()

    def device(step):
        return lax.rem(me + step + n_dom, n_dom)

    barrier = pltpu.get_barrier_semaphore()
    for step in STEPS:
        pl.semaphore_signal(barrier, inc=1, device_id={"dom": device(step)}, device_id_type=MESH)

    eye = iota((slots, slots), 0) == iota((slots, slots), 1)
    for c in loads[1:4]:
        c.wait()
    atom = jnp.sum(jnp.where(eye, slot_atom[...].astype(jnp.float32), 0.0), axis=1, keepdims=True)
    rank = atom_rank[...].astype(jnp.float32).reshape(1, atoms_all) + 1.0
    among = iota((slots, atoms_all), 1).astype(jnp.float32) == atom
    position = jnp.sum(jnp.where(among, rank, 0.0), axis=1, keepdims=True)
    place = iota((slots, LANES), 1)
    tables = []
    for b in range(5):
        owned = (place + device(b - 2) * atoms_dev + 1).astype(jnp.float32)
        tables.append(ones_where((owned == position) & (place < atoms_dev)))
    table = jnp.concatenate(tables, axis=1)
    windows[2] = jnp.zeros_like(windows[2])
    acc[...] = jnp.zeros_like(acc)

    loads[0].wait()
    pl.semaphore_wait(barrier, len(STEPS))

    def copy(k, src, dst, step):
        return pltpu.make_async_remote_copy(
            src_ref=src, dst_ref=dst, send_sem=send_sem.at[k], recv_sem=recv_sem.at[k],
            device_id={"dom": device(step)}, device_id_type=MESH,
        )

    halo = [
        copy(0, wave.at[:, planes - 2 : planes], low_halo, 1),
        copy(1, wave.at[:, 0:2], high_halo, -1),
    ]
    for c in halo:
        c.start()

    for n in range(bands):
        high, low = halves(wave[n].reshape(rows, nz).T)
        turned[n * nz : (n + 1) * nz, :] = high
        turned[wide + n * nz : wide + (n + 1) * nz, :] = low

    def gather(group, carry):
        for u in range(unroll):
            s = group * unroll + u
            flat = index[pl.ds(s, 1), :]
            hot = ones_where(
                iota((rows, pts), 0) == lax.shift_right_logical(flat, row_shift)
            ).astype(jnp.bfloat16)
            row_hot[s] = hot
            match = iota((nz, pts), 0) == (flat & lane_mask)
            col_hot[s] = ones_where(match).astype(jnp.bfloat16)
            lines = dot_dims(turned[...], hot, 1, 0)
            for n in range(bands):
                line = lines[n * nz : (n + 1) * nz] + lines[wide + n * nz : wide + (n + 1) * nz]
                line = jnp.where(match, line, 0.0)
                picked[n, pl.ds(s, 1), :] = jnp.sum(line, axis=0, keepdims=True)
        return carry

    lax.fori_loop(0, slots // unroll, gather, 0)

    loads[4].wait()
    same_slot = (iota((ns, si), 0) & (slots - 1)) == lax.shift_right_logical(iota((ns, si), 1), p_bits)
    same_band = lax.shift_right_logical(iota((ns, ni), 0), s_bits) == lax.shift_right_logical(
        iota((ns, ni), 1), p_bits
    )
    spread = ones_where((iota((ni, si), 0) & (nproj - 1)) == (iota((ni, si), 1) & (nproj - 1)))
    pairs = dot_full(picked[...].reshape(ns, pts), values[...], 1, 1)
    pairs = jnp.where(same_slot, pairs, 0.0)
    slot_rows = jnp.where(same_band, dot_hot(pairs, spread, 1, 1), 0.0)
    coeff = jnp.sum(slot_rows.reshape(bands, slots, ni), axis=0)
    partial = dot_hot(coeff.T, table, 1, 0)
    for b in range(5):
        parts[b] = partial[:, b * LANES : (b + 1) * LANES]

    first = [copy(2 + i, parts.at[step + 2], arrived.at[i], step) for i, step in enumerate(STEPS)]
    for c in first:
        c.start()

    def local(some):
        for n in some:
            for x in range(planes):
                f = wave[n, x]

                def plane(k):
                    if k < 0:
                        return low_halo[n, k + 2]
                    if k >= planes:
                        return high_halo[n, k - planes]
                    return wave[n, k]

                near = plane(x - 1) + plane(x + 1)
                far = plane(x - 2) + plane(x + 2)
                for axis, size in ((0, ny), (1, nz)):
                    near = near + pltpu.roll(f, 1, axis) + pltpu.roll(f, size - 1, axis)
                    far = far + pltpu.roll(f, 2, axis) + pltpu.roll(f, size - 2, axis)
                out[n, x] = (
                    (3.75 + potential[x] - energies[n]) * f - (2.0 / 3.0) * near + (1.0 / 24.0) * far
                )

    loads[7].wait()
    for c in halo:
        c.wait_recv()
    local(range(bands // 2))

    total = parts[2]
    for i, c in enumerate(first):
        c.wait_recv()
        total = total + arrived[i]

    for c in loads[5:7]:
        c.wait()
    for n in range(bands):
        matrix = d_part[...] - energies[n] * q_part[...]
        column = total[n * nproj : (n + 1) * nproj, :atoms_dev]
        windows[2, n * nproj : (n + 1) * nproj, :atoms_dev] = jnp.sum(matrix * column[None], axis=1)

    second = [copy(6 + i, windows.at[2], windows.at[step + 2], -step) for i, step in enumerate(STEPS)]
    for c in second:
        c.start()
    local(range(bands // 2, bands))
    for c in second:
        c.wait_recv()

    around = jnp.concatenate([windows[b] for b in range(5)], axis=1)
    slot_weight = dot_hot(around, table, 1, 1).T
    slot_weight = jnp.where(same_band, jnp.concatenate([slot_weight] * bands, axis=0), 0.0)
    blocks = jnp.where(same_slot, dot_hot(slot_weight, spread, 1, 0), 0.0)
    back_rows[...] = dot_full(blocks, values[...], 1, 0).reshape(bands, slots, pts)

    def scatter(group, carry):
        lefts, rights = [], []
        for u in range(unroll):
            s = group * unroll + u
            cols = col_hot[s].reshape(nz // 16, 16, pts)
            high_parts, low_parts = [], []
            for n in range(bands):
                line = jnp.broadcast_to(back_rows[n, pl.ds(s, 1), :], (16, pts))
                high, low = halves(line)
                high_parts.append((cols * high[None]).reshape(nz, pts))
                low_parts.append((cols * low[None]).reshape(nz, pts))
            lefts.append(jnp.concatenate(high_parts + low_parts, axis=0))
            rights.append(row_hot[s])
        acc[...] += dot_dims(jnp.concatenate(lefts, axis=1), jnp.concatenate(rights, axis=1), 1, 1)
        return carry

    lax.fori_loop(0, slots // unroll, scatter, 0)

    for n in range(bands):
        added = acc[n * nz : (n + 1) * nz, :] + acc[wide + n * nz : wide + (n + 1) * nz, :]
        out[n] += added.T.reshape(planes, ny, nz)

    for c in halo + first + second:
        c.wait_send()


def per_device(
    wave, potential, energies, proj_index, proj_values, slot_atom, atom_rank, d_matrix, q_matrix
):
    bands, planes, ny, nz = wave.shape
    slots, pts = proj_index.shape
    nproj = proj_values.shape[1]
    atoms_dev = d_matrix.shape[0]
    assert atoms_dev <= LANES and nz == LANES
    rows = planes * ny
    f32, bf16 = jnp.float32, jnp.bfloat16
    vmem = pl.BlockSpec(memory_space=pltpu.VMEM)
    atom_block = (bands * nproj, LANES)
    return pl.pallas_call(
        functools.partial(kernel, lax.axis_size("dom"), 4),
        out_shape=jax.ShapeDtypeStruct(wave.shape, f32),
        in_specs=[pl.BlockSpec(memory_space=pltpu.SMEM)]
        + [pl.BlockSpec(memory_space=pltpu.HBM)] * 8,
        out_specs=vmem,
        scratch_shapes=[
            pltpu.VMEM(wave.shape, f32),
            pltpu.VMEM(potential.shape, f32),
            pltpu.VMEM(proj_index.shape, jnp.int32),
            pltpu.VMEM((slots * nproj, pts), f32),
            pltpu.VMEM((1, slots), jnp.int32),
            pltpu.VMEM(atom_rank.shape, jnp.int32),
            pltpu.VMEM((nproj, nproj, atoms_dev), f32),
            pltpu.VMEM((nproj, nproj, atoms_dev), f32),
            pltpu.SemaphoreType.DMA((8,)),
            pltpu.VMEM((bands, 2, ny, nz), f32),
            pltpu.VMEM((bands, 2, ny, nz), f32),
            pltpu.VMEM((2 * bands * nz, rows), bf16),
            pltpu.VMEM((slots, rows, pts), bf16),
            pltpu.VMEM((slots, nz, pts), bf16),
            pltpu.VMEM((bands, slots, pts), f32),
            pltpu.VMEM((bands, slots, pts), f32),
            pltpu.VMEM((2 * bands * nz, rows), f32),
            pltpu.VMEM((5,) + atom_block, f32),
            pltpu.VMEM((4,) + atom_block, f32),
            pltpu.VMEM((5,) + atom_block, f32),
            pltpu.SemaphoreType.DMA((10,)),
            pltpu.SemaphoreType.DMA((10,)),
        ],
        compiler_params=pltpu.CompilerParams(
            collective_id=0, has_side_effects=True, vmem_limit_bytes=60 * 1024 * 1024
        ),
    )(
        energies, wave, potential, proj_index,
        proj_values.reshape(slots * nproj, pts),
        slot_atom.reshape(1, slots), atom_rank,
        jnp.transpose(d_matrix, (1, 2, 0)), jnp.transpose(q_matrix, (1, 2, 0)),
    )


def solution(mesh):
    placed = (
        P("band", "dom", None, None),
        P("dom", None, None),
        P("band"),
        P("dom", None),
        P("dom", None, None),
        P("dom"),
        P(),
        P("dom", None, None),
        P("dom", None, None),
    )
    return jax.shard_map(
        per_device,
        mesh=mesh,
        in_specs=placed,
        out_specs=P("band", "dom", None, None),
        check_vma=False,
    )
```

```python
import functools

import jax
import jax.numpy as jnp
from jax import lax
from jax.experimental import pallas as pl
from jax.experimental.pallas import tpu as pltpu
from jax.sharding import PartitionSpec as P

MESH = pl.DeviceIdType.MESH
STEPS = (-2, -1, 1, 2)
LANES = 128


def log2(size):
    bits = size.bit_length() - 1
    assert size == 1 << bits
    return bits


def iota(shape, dim):
    return lax.broadcasted_iota(jnp.int32, shape, dim)


def ones_where(mask):
    return jnp.where(mask, 1.0, 0.0).astype(jnp.float32)


def dot_dims(a, b, left, right):
    return lax.dot_general(
        a, b, (((left,), (right,)), ((), ())), preferred_element_type=jnp.float32
    )


def dot_hot(a, hot, left, right):
    high, low = halves(a)
    hot = hot.astype(jnp.bfloat16)
    return dot_dims(high, hot, left, right) + dot_dims(low, hot, left, right)


def dot_full(a, b, left, right):
    (a_high, a_low), (b_high, b_low) = halves(a), halves(b)
    return (
        dot_dims(a_high, b_high, left, right)
        + dot_dims(a_high, b_low, left, right)
        + dot_dims(a_low, b_high, left, right)
    )


def halves(value):
    high = value.astype(jnp.bfloat16)
    low = (value - high.astype(jnp.float32)).astype(jnp.bfloat16)
    return high, low


def kernel(
    n_dom, unroll,
    energies, wave_in, potential_in, index_in, values_in, slot_atom_in, atom_rank_in, d_in, q_in,
    out,
    wave, potential, index, values, slot_atom, atom_rank, d_part, q_part, load_sem,
    low_halo, high_halo, turned, row_hot, col_hot, picked, back_rows, acc,
    parts, arrived, windows, send_sem, recv_sem,
):
    bands, planes, ny, nz = wave.shape
    slots, pts = index.shape
    nproj = values.shape[0] // slots
    atoms_dev = d_part.shape[2]
    atoms_all = atom_rank.shape[0]
    ni, ns, si = bands * nproj, bands * slots, slots * nproj
    rows = planes * ny
    wide = bands * nz
    row_shift, lane_mask = log2(nz), nz - 1
    p_bits, s_bits = log2(nproj), log2(slots)

    me = lax.axis_index("dom")

    loads = [
        pltpu.make_async_copy(src, dst, load_sem.at[k])
        for k, (src, dst) in enumerate((
            (wave_in, wave), (index_in, index), (slot_atom_in, slot_atom),
            (atom_rank_in, atom_rank), (values_in, values), (d_in, d_part), (q_in, q_part),
            (potential_in, potential),
        ))
    ]
    for c in loads:
        c.start()

    def device(step):
        return lax.rem(me + step + n_dom, n_dom)

    barrier = pltpu.get_barrier_semaphore()
    for step in STEPS:
        pl.semaphore_signal(barrier, inc=1, device_id={"dom": device(step)}, device_id_type=MESH)

    eye = iota((slots, slots), 0) == iota((slots, slots), 1)
    for c in loads[1:4]:
        c.wait()
    atom = jnp.sum(jnp.where(eye, slot_atom[...].astype(jnp.float32), 0.0), axis=1, keepdims=True)
    rank = atom_rank[...].astype(jnp.float32).reshape(1, atoms_all) + 1.0
    among = iota((slots, atoms_all), 1).astype(jnp.float32) == atom
    position = jnp.sum(jnp.where(among, rank, 0.0), axis=1, keepdims=True)
    place = iota((slots, LANES), 1)
    tables = []
    for b in range(5):
        owned = (place + device(b - 2) * atoms_dev + 1).astype(jnp.float32)
        tables.append(ones_where((owned == position) & (place < atoms_dev)))
    table = jnp.concatenate(tables, axis=1)
    windows[2] = jnp.zeros_like(windows[2])
    acc[...] = jnp.zeros_like(acc)

    loads[0].wait()
    pl.semaphore_wait(barrier, len(STEPS))

    def copy(k, src, dst, step):
        return pltpu.make_async_remote_copy(
            src_ref=src, dst_ref=dst, send_sem=send_sem.at[k], recv_sem=recv_sem.at[k],
            device_id={"dom": device(step)}, device_id_type=MESH,
        )

    halo = [
        copy(0, wave.at[:, planes - 2 : planes], low_halo, 1),
        copy(1, wave.at[:, 0:2], high_halo, -1),
    ]
    for c in halo:
        c.start()

    for n in range(bands):
        high, low = halves(wave[n].reshape(rows, nz).T)
        turned[n * nz : (n + 1) * nz, :] = high
        turned[wide + n * nz : wide + (n + 1) * nz, :] = low

    def gather(group, carry):
        for u in range(unroll):
            s = group * unroll + u
            flat = index[pl.ds(s, 1), :]
            hot = ones_where(
                iota((rows, pts), 0) == lax.shift_right_logical(flat, row_shift)
            ).astype(jnp.bfloat16)
            match = iota((nz, pts), 0) == (flat & lane_mask)
            col_hot[s] = ones_where(match).astype(jnp.bfloat16)
            lines = dot_dims(turned[...], hot, 1, 0)
            for n in range(bands):
                line = lines[n * nz : (n + 1) * nz] + lines[wide + n * nz : wide + (n + 1) * nz]
                line = jnp.where(match, line, 0.0)
                picked[n, pl.ds(s, 1), :] = jnp.sum(line, axis=0, keepdims=True)
        return carry

    lax.fori_loop(0, slots // unroll, gather, 0)

    loads[4].wait()
    same_slot = (iota((ns, si), 0) & (slots - 1)) == lax.shift_right_logical(iota((ns, si), 1), p_bits)
    same_band = lax.shift_right_logical(iota((ns, ni), 0), s_bits) == lax.shift_right_logical(
        iota((ns, ni), 1), p_bits
    )
    spread = ones_where((iota((ni, si), 0) & (nproj - 1)) == (iota((ni, si), 1) & (nproj - 1)))
    pairs = dot_full(picked[...].reshape(ns, pts), values[...], 1, 1)
    pairs = jnp.where(same_slot, pairs, 0.0)
    slot_rows = jnp.where(same_band, dot_hot(pairs, spread, 1, 1), 0.0)
    coeff = jnp.sum(slot_rows.reshape(bands, slots, ni), axis=0)
    partial = dot_hot(coeff.T, table, 1, 0)
    for b in range(5):
        parts[b] = partial[:, b * LANES : (b + 1) * LANES]

    first = [copy(2 + i, parts.at[step + 2], arrived.at[i], step) for i, step in enumerate(STEPS)]
    for c in first:
        c.start()

    by_slot = lax.shift_right_logical(index[...], row_shift).astype(jnp.float32).T
    by_slot = by_slot.astype(jnp.bfloat16)

    def hots(group, carry):
        for u in range(unroll):
            s = group * unroll + u
            chosen = ones_where(iota((slots, rows), 0) == s).astype(jnp.bfloat16)
            spread_rows = dot_dims(by_slot, chosen, 1, 0)
            match = spread_rows == iota((pts, rows), 1).astype(jnp.float32)
            row_hot[s] = ones_where(match).astype(jnp.bfloat16)
        return carry

    def local(some):
        for n in some:
            for x in range(planes):
                f = wave[n, x]
                near, far = jnp.zeros_like(f), jnp.zeros_like(f)
                for axis, size in ((0, ny), (1, nz)):
                    near = near + pltpu.roll(f, 1, axis) + pltpu.roll(f, size - 1, axis)
                    far = far + pltpu.roll(f, 2, axis) + pltpu.roll(f, size - 2, axis)
                for k in (x - 1, x + 1):
                    if 0 <= k < planes:
                        near = near + wave[n, k]
                for k in (x - 2, x + 2):
                    if 0 <= k < planes:
                        far = far + wave[n, k]
                out[n, x] = (
                    (3.75 + potential[x] - energies[n]) * f - (2.0 / 3.0) * near + (1.0 / 24.0) * far
                )

    half = slots // unroll // 2
    lax.fori_loop(0, half, hots, 0)
    loads[7].wait()
    local(range(bands // 2))

    total = parts[2]
    for i, c in enumerate(first):
        c.wait_recv()
        total = total + arrived[i]

    for c in loads[5:7]:
        c.wait()
    for n in range(bands):
        matrix = d_part[...] - energies[n] * q_part[...]
        column = total[n * nproj : (n + 1) * nproj, :atoms_dev]
        windows[2, n * nproj : (n + 1) * nproj, :atoms_dev] = jnp.sum(matrix * column[None], axis=1)

    second = [copy(6 + i, windows.at[2], windows.at[step + 2], -step) for i, step in enumerate(STEPS)]
    for c in second:
        c.start()
    lax.fori_loop(half, slots // unroll, hots, 0)
    local(range(bands // 2, bands))
    for c in second:
        c.wait_recv()

    around = jnp.concatenate([windows[b] for b in range(5)], axis=1)
    slot_weight = dot_hot(around, table, 1, 1).T
    slot_weight = jnp.where(same_band, jnp.concatenate([slot_weight] * bands, axis=0), 0.0)
    blocks = jnp.where(same_slot, dot_hot(slot_weight, spread, 1, 0), 0.0)
    back_rows[...] = dot_full(blocks, values[...], 1, 0).reshape(bands, slots, pts)

    def scatter(group, carry):
        lefts, rights = [], []
        for u in range(unroll):
            s = group * unroll + u
            cols = col_hot[s].reshape(nz // 16, 16, pts)
            high_parts, low_parts = [], []
            for n in range(bands):
                line = jnp.broadcast_to(back_rows[n, pl.ds(s, 1), :], (16, pts))
                high, low = halves(line)
                high_parts.append((cols * high[None]).reshape(nz, pts))
                low_parts.append((cols * low[None]).reshape(nz, pts))
            lefts.append(jnp.concatenate(high_parts + low_parts, axis=0))
            rights.append(row_hot[s])
        acc[...] += dot_dims(jnp.concatenate(lefts, axis=1), jnp.concatenate(rights, axis=0), 1, 0)
        return carry

    lax.fori_loop(0, slots // unroll, scatter, 0)

    for c in halo:
        c.wait_recv()

    def beyond(n, k):
        return low_halo[n, k + 2] if k < 0 else high_halo[n, k - planes]

    for n in range(bands):
        added = acc[n * nz : (n + 1) * nz, :] + acc[wide + n * nz : wide + (n + 1) * nz, :]
        added = added.T.reshape(planes, ny, nz)
        for x in range(planes):
            plane = out[n, x] + added[x]
            for distance, factor in ((1, -2.0 / 3.0), (2, 1.0 / 24.0)):
                for k in (x - distance, x + distance):
                    if not 0 <= k < planes:
                        plane = plane + factor * beyond(n, k)
            out[n, x] = plane

    for c in halo + first + second:
        c.wait_send()


def per_device(
    wave, potential, energies, proj_index, proj_values, slot_atom, atom_rank, d_matrix, q_matrix
):
    bands, planes, ny, nz = wave.shape
    slots, pts = proj_index.shape
    nproj = proj_values.shape[1]
    atoms_dev = d_matrix.shape[0]
    assert atoms_dev <= LANES and nz == LANES
    rows = planes * ny
    f32, bf16 = jnp.float32, jnp.bfloat16
    vmem = pl.BlockSpec(memory_space=pltpu.VMEM)
    atom_block = (bands * nproj, LANES)
    return pl.pallas_call(
        functools.partial(kernel, lax.axis_size("dom"), 4),
        out_shape=jax.ShapeDtypeStruct(wave.shape, f32),
        in_specs=[pl.BlockSpec(memory_space=pltpu.SMEM)]
        + [pl.BlockSpec(memory_space=pltpu.HBM)] * 8,
        out_specs=vmem,
        scratch_shapes=[
            pltpu.VMEM(wave.shape, f32),
            pltpu.VMEM(potential.shape, f32),
            pltpu.VMEM(proj_index.shape, jnp.int32),
            pltpu.VMEM((slots * nproj, pts), f32),
            pltpu.VMEM((1, slots), jnp.int32),
            pltpu.VMEM(atom_rank.shape, jnp.int32),
            pltpu.VMEM((nproj, nproj, atoms_dev), f32),
            pltpu.VMEM((nproj, nproj, atoms_dev), f32),
            pltpu.SemaphoreType.DMA((8,)),
            pltpu.VMEM((bands, 2, ny, nz), f32),
            pltpu.VMEM((bands, 2, ny, nz), f32),
            pltpu.VMEM((2 * bands * nz, rows), bf16),
            pltpu.VMEM((slots, pts, rows), bf16),
            pltpu.VMEM((slots, nz, pts), bf16),
            pltpu.VMEM((bands, slots, pts), f32),
            pltpu.VMEM((bands, slots, pts), f32),
            pltpu.VMEM((2 * bands * nz, rows), f32),
            pltpu.VMEM((5,) + atom_block, f32),
            pltpu.VMEM((4,) + atom_block, f32),
            pltpu.VMEM((5,) + atom_block, f32),
            pltpu.SemaphoreType.DMA((10,)),
            pltpu.SemaphoreType.DMA((10,)),
        ],
        compiler_params=pltpu.CompilerParams(
            collective_id=0, has_side_effects=True, vmem_limit_bytes=60 * 1024 * 1024
        ),
    )(
        energies, wave, potential, proj_index,
        proj_values.reshape(slots * nproj, pts),
        slot_atom.reshape(1, slots), atom_rank,
        jnp.transpose(d_matrix, (1, 2, 0)), jnp.transpose(q_matrix, (1, 2, 0)),
    )


def solution(mesh):
    placed = (
        P("band", "dom", None, None),
        P("dom", None, None),
        P("band"),
        P("dom", None),
        P("dom", None, None),
        P("dom"),
        P(),
        P("dom", None, None),
        P("dom", None, None),
    )
    return jax.shard_map(
        per_device,
        mesh=mesh,
        in_specs=placed,
        out_specs=P("band", "dom", None, None),
        check_vma=False,
    )
```

```python
import functools

import jax
import jax.numpy as jnp
from jax import lax
from jax.experimental import pallas as pl
from jax.experimental.pallas import tpu as pltpu
from jax.sharding import PartitionSpec as P

MESH = pl.DeviceIdType.MESH
STEPS = (-2, -1, 1, 2)
LANES = 128


def log2(size):
    bits = size.bit_length() - 1
    assert size == 1 << bits
    return bits


def iota(shape, dim):
    return lax.broadcasted_iota(jnp.int32, shape, dim)


def ones_where(mask):
    return jnp.where(mask, 1.0, 0.0).astype(jnp.float32)


def dot_dims(a, b, left, right):
    return lax.dot_general(
        a, b, (((left,), (right,)), ((), ())), preferred_element_type=jnp.float32
    )


def dot_hot(a, hot, left, right):
    high, low = halves(a)
    hot = hot.astype(jnp.bfloat16)
    return dot_dims(high, hot, left, right) + dot_dims(low, hot, left, right)


def dot_full(a, b, left, right):
    (a_high, a_low), (b_high, b_low) = halves(a), halves(b)
    return (
        dot_dims(a_high, b_high, left, right)
        + dot_dims(a_high, b_low, left, right)
        + dot_dims(a_low, b_high, left, right)
    )


def halves(value):
    high = value.astype(jnp.bfloat16)
    low = (value - high.astype(jnp.float32)).astype(jnp.bfloat16)
    return high, low


def kernel(
    n_dom, unroll,
    energies, wave_in, index_in, values_in, slot_atom_in, atom_rank_in, d_in, q_in,
    out,
    wave, index, values, slot_atom, atom_rank, d_part, q_part, load_sem,
    low_halo, high_halo, turned, row_hot, col_hot, picked, back_rows, acc,
    parts, arrived, windows, send_sem, recv_sem,
):
    bands, planes, ny, nz = wave.shape
    slots, pts = index.shape
    nproj = values.shape[0] // slots
    atoms_dev = d_part.shape[2]
    atoms_all = atom_rank.shape[0]
    ni, ns, si = bands * nproj, bands * slots, slots * nproj
    rows = planes * ny
    wide = bands * nz
    row_shift, lane_mask = log2(nz), nz - 1
    p_bits, s_bits = log2(nproj), log2(slots)

    me = lax.axis_index("dom")

    loads = [
        pltpu.make_async_copy(src, dst, load_sem.at[k])
        for k, (src, dst) in enumerate((
            (wave_in, wave), (index_in, index), (slot_atom_in, slot_atom),
            (atom_rank_in, atom_rank), (values_in, values), (d_in, d_part), (q_in, q_part),
        ))
    ]
    for c in loads:
        c.start()

    def device(step):
        return lax.rem(me + step + n_dom, n_dom)

    barrier = pltpu.get_barrier_semaphore()
    for step in STEPS:
        pl.semaphore_signal(barrier, inc=1, device_id={"dom": device(step)}, device_id_type=MESH)

    eye = iota((slots, slots), 0) == iota((slots, slots), 1)
    for c in loads[1:4]:
        c.wait()
    atom = jnp.sum(jnp.where(eye, slot_atom[...].astype(jnp.float32), 0.0), axis=1, keepdims=True)
    rank = atom_rank[...].astype(jnp.float32).reshape(1, atoms_all) + 1.0
    among = iota((slots, atoms_all), 1).astype(jnp.float32) == atom
    position = jnp.sum(jnp.where(among, rank, 0.0), axis=1, keepdims=True)
    place = iota((slots, LANES), 1)
    tables = []
    for b in range(5):
        owned = (place + device(b - 2) * atoms_dev + 1).astype(jnp.float32)
        tables.append(ones_where((owned == position) & (place < atoms_dev)))
    table = jnp.concatenate(tables, axis=1)
    windows[2] = jnp.zeros_like(windows[2])
    acc[...] = jnp.zeros_like(acc)

    loads[0].wait()
    pl.semaphore_wait(barrier, len(STEPS))

    def copy(k, src, dst, step):
        return pltpu.make_async_remote_copy(
            src_ref=src, dst_ref=dst, send_sem=send_sem.at[k], recv_sem=recv_sem.at[k],
            device_id={"dom": device(step)}, device_id_type=MESH,
        )

    halo = [
        copy(0, wave.at[:, planes - 2 : planes], low_halo, 1),
        copy(1, wave.at[:, 0:2], high_halo, -1),
    ]
    for c in halo:
        c.start()

    for n in range(bands):
        high, low = halves(wave[n].reshape(rows, nz).T)
        turned[n * nz : (n + 1) * nz, :] = high
        turned[wide + n * nz : wide + (n + 1) * nz, :] = low

    def gather(group, carry):
        for u in range(unroll):
            s = group * unroll + u
            flat = index[pl.ds(s, 1), :]
            hot = ones_where(
                iota((rows, pts), 0) == lax.shift_right_logical(flat, row_shift)
            ).astype(jnp.bfloat16)
            match = iota((nz, pts), 0) == (flat & lane_mask)
            col_hot[s] = ones_where(match).astype(jnp.bfloat16)
            lines = dot_dims(turned[...], hot, 1, 0)
            for n in range(bands):
                line = lines[n * nz : (n + 1) * nz] + lines[wide + n * nz : wide + (n + 1) * nz]
                line = jnp.where(match, line, 0.0)
                picked[n, pl.ds(s, 1), :] = jnp.sum(line, axis=0, keepdims=True)
        return carry

    lax.fori_loop(0, slots // unroll, gather, 0)

    loads[4].wait()
    same_slot = (iota((ns, si), 0) & (slots - 1)) == lax.shift_right_logical(iota((ns, si), 1), p_bits)
    same_band = lax.shift_right_logical(iota((ns, ni), 0), s_bits) == lax.shift_right_logical(
        iota((ns, ni), 1), p_bits
    )
    spread = ones_where((iota((ni, si), 0) & (nproj - 1)) == (iota((ni, si), 1) & (nproj - 1)))
    pairs = dot_full(picked[...].reshape(ns, pts), values[...], 1, 1)
    pairs = jnp.where(same_slot, pairs, 0.0)
    slot_rows = jnp.where(same_band, dot_hot(pairs, spread, 1, 1), 0.0)
    coeff = jnp.sum(slot_rows.reshape(bands, slots, ni), axis=0)
    partial = dot_hot(coeff.T, table, 1, 0)
    for b in range(5):
        parts[b] = partial[:, b * LANES : (b + 1) * LANES]

    first = [copy(2 + i, parts.at[step + 2], arrived.at[i], step) for i, step in enumerate(STEPS)]
    for c in first:
        c.start()

    by_slot = lax.shift_right_logical(index[...], row_shift).astype(jnp.float32).T
    by_slot = by_slot.astype(jnp.bfloat16)

    def hots(group, carry):
        for u in range(unroll):
            s = group * unroll + u
            chosen = ones_where(iota((slots, rows), 0) == s).astype(jnp.bfloat16)
            spread_rows = dot_dims(by_slot, chosen, 1, 0)
            match = spread_rows == iota((pts, rows), 1).astype(jnp.float32)
            row_hot[s] = ones_where(match).astype(jnp.bfloat16)
        return carry

    def local(some):
        for n in some:
            for x in range(planes):
                f = wave[n, x]
                near, far = jnp.zeros_like(f), jnp.zeros_like(f)
                for axis, size in ((0, ny), (1, nz)):
                    near = near + pltpu.roll(f, 1, axis) + pltpu.roll(f, size - 1, axis)
                    far = far + pltpu.roll(f, 2, axis) + pltpu.roll(f, size - 2, axis)
                for k in (x - 1, x + 1):
                    if 0 <= k < planes:
                        near = near + wave[n, k]
                for k in (x - 2, x + 2):
                    if 0 <= k < planes:
                        far = far + wave[n, k]
                out[n, x] = 3.75 * f - (2.0 / 3.0) * near + (1.0 / 24.0) * far

    half = slots // unroll // 2
    lax.fori_loop(0, half, hots, 0)
    local(range(bands // 2))

    total = parts[2]
    for i, c in enumerate(first):
        c.wait_recv()
        total = total + arrived[i]

    for c in loads[5:7]:
        c.wait()
    for n in range(bands):
        matrix = d_part[...] - energies[n] * q_part[...]
        column = total[n * nproj : (n + 1) * nproj, :atoms_dev]
        windows[2, n * nproj : (n + 1) * nproj, :atoms_dev] = jnp.sum(matrix * column[None], axis=1)

    second = [copy(6 + i, windows.at[2], windows.at[step + 2], -step) for i, step in enumerate(STEPS)]
    for c in second:
        c.start()
    lax.fori_loop(half, slots // unroll, hots, 0)
    local(range(bands // 2, bands))
    for c in second:
        c.wait_recv()

    around = jnp.concatenate([windows[b] for b in range(5)], axis=1)
    slot_weight = dot_hot(around, table, 1, 1).T
    slot_weight = jnp.where(same_band, jnp.concatenate([slot_weight] * bands, axis=0), 0.0)
    blocks = jnp.where(same_slot, dot_hot(slot_weight, spread, 1, 0), 0.0)
    back_rows[...] = dot_full(blocks, values[...], 1, 0).reshape(bands, slots, pts)

    def scatter(group, carry):
        lefts, rights = [], []
        for u in range(unroll):
            s = group * unroll + u
            cols = col_hot[s].reshape(nz // 16, 16, pts)
            high_parts, low_parts = [], []
            for n in range(bands):
                line = jnp.broadcast_to(back_rows[n, pl.ds(s, 1), :], (16, pts))
                high, low = halves(line)
                high_parts.append((cols * high[None]).reshape(nz, pts))
                low_parts.append((cols * low[None]).reshape(nz, pts))
            lefts.append(jnp.concatenate(high_parts + low_parts, axis=0))
            rights.append(row_hot[s])
        acc[...] += dot_dims(jnp.concatenate(lefts, axis=1), jnp.concatenate(rights, axis=0), 1, 0)
        return carry

    lax.fori_loop(0, slots // unroll, scatter, 0)

    for c in halo:
        c.wait_recv()

    def beyond(n, k):
        return low_halo[n, k + 2] if k < 0 else high_halo[n, k - planes]

    for n in range(bands):
        added = acc[n * nz : (n + 1) * nz, :] + acc[wide + n * nz : wide + (n + 1) * nz, :]
        added = added.T.reshape(planes, ny, nz)
        for x in range(planes):
            plane = out[n, x] + added[x]
            for distance, factor in ((1, -2.0 / 3.0), (2, 1.0 / 24.0)):
                for k in (x - distance, x + distance):
                    if not 0 <= k < planes:
                        plane = plane + factor * beyond(n, k)
            out[n, x] = plane

    for c in halo + first + second:
        c.wait_send()


def per_device(
    wave, potential, energies, proj_index, proj_values, slot_atom, atom_rank, d_matrix, q_matrix
):
    bands, planes, ny, nz = wave.shape
    slots, pts = proj_index.shape
    nproj = proj_values.shape[1]
    atoms_dev = d_matrix.shape[0]
    assert atoms_dev <= LANES and nz == LANES
    rows = planes * ny
    f32, bf16 = jnp.float32, jnp.bfloat16
    vmem = pl.BlockSpec(memory_space=pltpu.VMEM)
    atom_block = (bands * nproj, LANES)
    rest = pl.pallas_call(
        functools.partial(kernel, lax.axis_size("dom"), 4),
        out_shape=jax.ShapeDtypeStruct(wave.shape, f32),
        in_specs=[pl.BlockSpec(memory_space=pltpu.SMEM)]
        + [pl.BlockSpec(memory_space=pltpu.HBM)] * 7,
        out_specs=vmem,
        scratch_shapes=[
            pltpu.VMEM(wave.shape, f32),
            pltpu.VMEM(proj_index.shape, jnp.int32),
            pltpu.VMEM((slots * nproj, pts), f32),
            pltpu.VMEM((1, slots), jnp.int32),
            pltpu.VMEM(atom_rank.shape, jnp.int32),
            pltpu.VMEM((nproj, nproj, atoms_dev), f32),
            pltpu.VMEM((nproj, nproj, atoms_dev), f32),
            pltpu.SemaphoreType.DMA((7,)),
            pltpu.VMEM((bands, 2, ny, nz), f32),
            pltpu.VMEM((bands, 2, ny, nz), f32),
            pltpu.VMEM((2 * bands * nz, rows), bf16),
            pltpu.VMEM((slots, pts, rows), bf16),
            pltpu.VMEM((slots, nz, pts), bf16),
            pltpu.VMEM((bands, slots, pts), f32),
            pltpu.VMEM((bands, slots, pts), f32),
            pltpu.VMEM((2 * bands * nz, rows), f32),
            pltpu.VMEM((5,) + atom_block, f32),
            pltpu.VMEM((4,) + atom_block, f32),
            pltpu.VMEM((5,) + atom_block, f32),
            pltpu.SemaphoreType.DMA((10,)),
            pltpu.SemaphoreType.DMA((10,)),
        ],
        compiler_params=pltpu.CompilerParams(
            collective_id=0, has_side_effects=True, vmem_limit_bytes=60 * 1024 * 1024
        ),
    )(
        energies, wave, proj_index,
        proj_values.reshape(slots * nproj, pts),
        slot_atom.reshape(1, slots), atom_rank,
        jnp.transpose(d_matrix, (1, 2, 0)), jnp.transpose(q_matrix, (1, 2, 0)),
    )
    return rest + (potential[None] - energies[:, None, None, None]) * wave


def solution(mesh):
    placed = (
        P("band", "dom", None, None),
        P("dom", None, None),
        P("band"),
        P("dom", None),
        P("dom", None, None),
        P("dom"),
        P(),
        P("dom", None, None),
        P("dom", None, None),
    )
    return jax.shard_map(
        per_device,
        mesh=mesh,
        in_specs=placed,
        out_specs=P("band", "dom", None, None),
        check_vma=False,
    )
```

```python
import functools

import jax
import jax.numpy as jnp
from jax import lax
from jax.experimental import pallas as pl
from jax.experimental.pallas import tpu as pltpu
from jax.sharding import PartitionSpec as P

MESH = pl.DeviceIdType.MESH
STEPS = (-2, -1, 1, 2)
LANES = 128


def log2(size):
    bits = size.bit_length() - 1
    assert size == 1 << bits
    return bits


def iota(shape, dim):
    return lax.broadcasted_iota(jnp.int32, shape, dim)


def ones_where(mask):
    return jnp.where(mask, 1.0, 0.0).astype(jnp.float32)


def dot_dims(a, b, left, right):
    return lax.dot_general(
        a, b, (((left,), (right,)), ((), ())), preferred_element_type=jnp.float32
    )


def dot_hot(a, hot, left, right):
    high, low = halves(a)
    hot = hot.astype(jnp.bfloat16)
    return dot_dims(high, hot, left, right) + dot_dims(low, hot, left, right)


def dot_full(a, b, left, right):
    (a_high, a_low), (b_high, b_low) = halves(a), halves(b)
    return (
        dot_dims(a_high, b_high, left, right)
        + dot_dims(a_high, b_low, left, right)
        + dot_dims(a_low, b_high, left, right)
    )


def halves(value):
    high = value.astype(jnp.bfloat16)
    low = (value - high.astype(jnp.float32)).astype(jnp.bfloat16)
    return high, low


def kernel(
    n_dom, unroll,
    energies, wave_in, potential_in, index_in, values_in, slot_atom_in, atom_rank_in, d_in, q_in,
    out,
    wave, potential, index, values, slot_atom, atom_rank, d_part, q_part, load_sem,
    low_halo, high_halo, turned, row_hot, col_hot, picked, back_rows, acc,
    parts, arrived, windows, send_sem, recv_sem,
):
    bands, planes, ny, nz = wave.shape
    slots, pts = index.shape
    nproj = values.shape[0] // slots
    atoms_dev = d_part.shape[2]
    atoms_all = atom_rank.shape[0]
    ni, ns, si = bands * nproj, bands * slots, slots * nproj
    rows = planes * ny
    wide = bands * nz
    row_shift, lane_mask = log2(nz), nz - 1
    p_bits, s_bits = log2(nproj), log2(slots)

    me = lax.axis_index("dom")

    loads = [
        pltpu.make_async_copy(src, dst, load_sem.at[k])
        for k, (src, dst) in enumerate((
            (wave_in, wave), (index_in, index), (slot_atom_in, slot_atom),
            (atom_rank_in, atom_rank), (values_in, values), (d_in, d_part), (q_in, q_part),
            (potential_in, potential),
        ))
    ]
    for c in loads:
        c.start()

    def device(step):
        return lax.rem(me + step + n_dom, n_dom)

    barrier = pltpu.get_barrier_semaphore()
    for step in STEPS:
        pl.semaphore_signal(barrier, inc=1, device_id={"dom": device(step)}, device_id_type=MESH)

    eye = iota((slots, slots), 0) == iota((slots, slots), 1)
    for c in loads[1:4]:
        c.wait()
    atom = jnp.sum(jnp.where(eye, slot_atom[...].astype(jnp.float32), 0.0), axis=1, keepdims=True)
    rank = atom_rank[...].astype(jnp.float32).reshape(1, atoms_all) + 1.0
    among = iota((slots, atoms_all), 1).astype(jnp.float32) == atom
    position = jnp.sum(jnp.where(among, rank, 0.0), axis=1, keepdims=True)
    place = iota((slots, LANES), 1)
    tables = []
    for b in range(5):
        owned = (place + device(b - 2) * atoms_dev + 1).astype(jnp.float32)
        tables.append(ones_where((owned == position) & (place < atoms_dev)))
    table = jnp.concatenate(tables, axis=1)
    windows[2] = jnp.zeros_like(windows[2])
    acc[...] = jnp.zeros_like(acc)

    loads[0].wait()
    pl.semaphore_wait(barrier, len(STEPS))

    def copy(k, src, dst, step):
        return pltpu.make_async_remote_copy(
            src_ref=src, dst_ref=dst, send_sem=send_sem.at[k], recv_sem=recv_sem.at[k],
            device_id={"dom": device(step)}, device_id_type=MESH,
        )

    halo = [
        copy(0, wave.at[:, planes - 2 : planes], low_halo, 1),
        copy(1, wave.at[:, 0:2], high_halo, -1),
    ]
    for c in halo:
        c.start()

    for n in range(bands):
        high, low = halves(wave[n].reshape(rows, nz).T)
        turned[n * nz : (n + 1) * nz, :] = high
        turned[wide + n * nz : wide + (n + 1) * nz, :] = low

    def gather(group, carry):
        for u in range(unroll):
            s = group * unroll + u
            flat = index[pl.ds(s, 1), :]
            hot = ones_where(
                iota((rows, pts), 0) == lax.shift_right_logical(flat, row_shift)
            ).astype(jnp.bfloat16)
            match = iota((nz, pts), 0) == (flat & lane_mask)
            col_hot[s] = ones_where(match).astype(jnp.bfloat16)
            lines = dot_dims(turned[...], hot, 1, 0)
            for n in range(bands):
                line = lines[n * nz : (n + 1) * nz] + lines[wide + n * nz : wide + (n + 1) * nz]
                line = jnp.where(match, line, 0.0)
                picked[n, pl.ds(s, 1), :] = jnp.sum(line, axis=0, keepdims=True)
        return carry

    lax.fori_loop(0, slots // unroll, gather, 0)

    loads[4].wait()
    same_slot = (iota((ns, si), 0) & (slots - 1)) == lax.shift_right_logical(iota((ns, si), 1), p_bits)
    same_band = lax.shift_right_logical(iota((ns, ni), 0), s_bits) == lax.shift_right_logical(
        iota((ns, ni), 1), p_bits
    )
    spread = ones_where((iota((ni, si), 0) & (nproj - 1)) == (iota((ni, si), 1) & (nproj - 1)))
    pairs = dot_full(picked[...].reshape(ns, pts), values[...], 1, 1)
    pairs = jnp.where(same_slot, pairs, 0.0)
    slot_rows = jnp.where(same_band, dot_hot(pairs, spread, 1, 1), 0.0)
    coeff = jnp.sum(slot_rows.reshape(bands, slots, ni), axis=0)
    partial = dot_hot(coeff.T, table, 1, 0)
    for b in range(5):
        parts[b] = partial[:, b * LANES : (b + 1) * LANES]

    first = [copy(2 + i, parts.at[step + 2], arrived.at[i], step) for i, step in enumerate(STEPS)]
    for c in first:
        c.start()

    by_slot = lax.shift_right_logical(index[...], row_shift).astype(jnp.float32).T
    by_slot = by_slot.astype(jnp.bfloat16)

    def hots(group, carry):
        for u in range(unroll):
            s = group * unroll + u
            chosen = ones_where(iota((slots, rows), 0) == s).astype(jnp.bfloat16)
            spread_rows = dot_dims(by_slot, chosen, 1, 0)
            match = spread_rows == iota((pts, rows), 1).astype(jnp.float32)
            row_hot[s] = ones_where(match).astype(jnp.bfloat16)
        return carry

    def local(some):
        for n in some:
            for x in range(planes):
                f = wave[n, x]
                near, far = jnp.zeros_like(f), jnp.zeros_like(f)
                for axis, size in ((0, ny), (1, nz)):
                    near = near + pltpu.roll(f, 1, axis) + pltpu.roll(f, size - 1, axis)
                    far = far + pltpu.roll(f, 2, axis) + pltpu.roll(f, size - 2, axis)
                for k in (x - 1, x + 1):
                    if 0 <= k < planes:
                        near = near + wave[n, k]
                for k in (x - 2, x + 2):
                    if 0 <= k < planes:
                        far = far + wave[n, k]
                out[n, x] = (
                    (3.75 + potential[x] - energies[n]) * f - (2.0 / 3.0) * near + (1.0 / 24.0) * far
                )

    half = slots // unroll // 2
    lax.fori_loop(0, half, hots, 0)
    loads[7].wait()
    local(range(bands // 2))

    total = parts[2]
    for i, c in enumerate(first):
        c.wait_recv()
        total = total + arrived[i]

    for c in loads[5:7]:
        c.wait()
    for n in range(bands):
        matrix = d_part[...] - energies[n] * q_part[...]
        column = total[n * nproj : (n + 1) * nproj, :atoms_dev]
        windows[2, n * nproj : (n + 1) * nproj, :atoms_dev] = jnp.sum(matrix * column[None], axis=1)

    second = [copy(6 + i, windows.at[2], windows.at[step + 2], -step) for i, step in enumerate(STEPS)]
    for c in second:
        c.start()
    lax.fori_loop(half, slots // unroll, hots, 0)
    local(range(bands // 2, bands))
    for c in second:
        c.wait_recv()

    around = jnp.concatenate([windows[b] for b in range(5)], axis=1)
    slot_weight = dot_hot(around, table, 1, 1).T
    slot_weight = jnp.where(same_band, jnp.concatenate([slot_weight] * bands, axis=0), 0.0)
    blocks = jnp.where(same_slot, dot_hot(slot_weight, spread, 1, 0), 0.0)
    back_rows[...] = dot_full(blocks, values[...], 1, 0).reshape(bands, slots, pts)

    def scatter(group, carry):
        lefts, rights = [], []
        for u in range(unroll):
            s = group * unroll + u
            cols = col_hot[s].reshape(nz // 16, 16, pts)
            high_parts, low_parts = [], []
            for n in range(bands):
                line = jnp.broadcast_to(back_rows[n, pl.ds(s, 1), :], (16, pts))
                high, low = halves(line)
                high_parts.append((cols * high[None]).reshape(nz, pts))
                low_parts.append((cols * low[None]).reshape(nz, pts))
            lefts.append(jnp.concatenate(high_parts + low_parts, axis=0))
            rights.append(row_hot[s])
        acc[...] += dot_dims(jnp.concatenate(lefts, axis=1), jnp.concatenate(rights, axis=0), 1, 0)
        return carry

    lax.fori_loop(0, slots // unroll, scatter, 0)

    for c in halo:
        c.wait_recv()

    def beyond(n, k):
        return low_halo[n, k + 2] if k < 0 else high_halo[n, k - planes]

    for n in range(bands):
        added = acc[n * nz : (n + 1) * nz, :] + acc[wide + n * nz : wide + (n + 1) * nz, :]
        added = added.T.reshape(planes, ny, nz)
        for x in range(planes):
            plane = out[n, x] + added[x]
            for distance, factor in ((1, -2.0 / 3.0), (2, 1.0 / 24.0)):
                for k in (x - distance, x + distance):
                    if not 0 <= k < planes:
                        plane = plane + factor * beyond(n, k)
            out[n, x] = plane

    for c in halo + first + second:
        c.wait_send()


def per_device(
    wave, potential, energies, proj_index, proj_values, slot_atom, atom_rank, d_matrix, q_matrix
):
    bands, planes, ny, nz = wave.shape
    slots, pts = proj_index.shape
    nproj = proj_values.shape[1]
    atoms_dev = d_matrix.shape[0]
    assert atoms_dev <= LANES and nz == LANES
    rows = planes * ny
    f32, bf16 = jnp.float32, jnp.bfloat16
    vmem = pl.BlockSpec(memory_space=pltpu.VMEM)
    atom_block = (bands * nproj, LANES)
    return pl.pallas_call(
        functools.partial(kernel, lax.axis_size("dom"), 8),
        out_shape=jax.ShapeDtypeStruct(wave.shape, f32),
        in_specs=[pl.BlockSpec(memory_space=pltpu.SMEM)]
        + [pl.BlockSpec(memory_space=pltpu.HBM)] * 8,
        out_specs=vmem,
        scratch_shapes=[
            pltpu.VMEM(wave.shape, f32),
            pltpu.VMEM(potential.shape, f32),
            pltpu.VMEM(proj_index.shape, jnp.int32),
            pltpu.VMEM((slots * nproj, pts), f32),
            pltpu.VMEM((1, slots), jnp.int32),
            pltpu.VMEM(atom_rank.shape, jnp.int32),
            pltpu.VMEM((nproj, nproj, atoms_dev), f32),
            pltpu.VMEM((nproj, nproj, atoms_dev), f32),
            pltpu.SemaphoreType.DMA((8,)),
            pltpu.VMEM((bands, 2, ny, nz), f32),
            pltpu.VMEM((bands, 2, ny, nz), f32),
            pltpu.VMEM((2 * bands * nz, rows), bf16),
            pltpu.VMEM((slots, pts, rows), bf16),
            pltpu.VMEM((slots, nz, pts), bf16),
            pltpu.VMEM((bands, slots, pts), f32),
            pltpu.VMEM((bands, slots, pts), f32),
            pltpu.VMEM((2 * bands * nz, rows), f32),
            pltpu.VMEM((5,) + atom_block, f32),
            pltpu.VMEM((4,) + atom_block, f32),
            pltpu.VMEM((5,) + atom_block, f32),
            pltpu.SemaphoreType.DMA((10,)),
            pltpu.SemaphoreType.DMA((10,)),
        ],
        compiler_params=pltpu.CompilerParams(
            collective_id=0, has_side_effects=True, vmem_limit_bytes=60 * 1024 * 1024
        ),
    )(
        energies, wave, potential, proj_index,
        proj_values.reshape(slots * nproj, pts),
        slot_atom.reshape(1, slots), atom_rank,
        jnp.transpose(d_matrix, (1, 2, 0)), jnp.transpose(q_matrix, (1, 2, 0)),
    )


def solution(mesh):
    placed = (
        P("band", "dom", None, None),
        P("dom", None, None),
        P("band"),
        P("dom", None),
        P("dom", None, None),
        P("dom"),
        P(),
        P("dom", None, None),
        P("dom", None, None),
    )
    return jax.shard_map(
        per_device,
        mesh=mesh,
        in_specs=placed,
        out_specs=P("band", "dom", None, None),
        check_vma=False,
    )
```

```python
import functools

import jax
import jax.numpy as jnp
from jax import lax
from jax.experimental import pallas as pl
from jax.experimental.pallas import tpu as pltpu
from jax.sharding import PartitionSpec as P

MESH = pl.DeviceIdType.MESH
STEPS = (-2, -1, 1, 2)
LANES = 128


def log2(size):
    bits = size.bit_length() - 1
    assert size == 1 << bits
    return bits


def iota(shape, dim):
    return lax.broadcasted_iota(jnp.int32, shape, dim)


def ones_where(mask):
    return jnp.where(mask, 1.0, 0.0).astype(jnp.float32)


def dot_dims(a, b, left, right):
    return lax.dot_general(
        a, b, (((left,), (right,)), ((), ())), preferred_element_type=jnp.float32
    )


def dot_hot(a, hot, left, right):
    high, low = halves(a)
    hot = hot.astype(jnp.bfloat16)
    return dot_dims(high, hot, left, right) + dot_dims(low, hot, left, right)


def dot_full(a, b, left, right):
    (a_high, a_low), (b_high, b_low) = halves(a), halves(b)
    return (
        dot_dims(a_high, b_high, left, right)
        + dot_dims(a_high, b_low, left, right)
        + dot_dims(a_low, b_high, left, right)
    )


def halves(value):
    high = value.astype(jnp.bfloat16)
    low = (value - high.astype(jnp.float32)).astype(jnp.bfloat16)
    return high, low


def kernel(
    n_dom, unroll,
    energies, wave_in, potential_in, index_in, values_in, slot_atom_in, atom_rank_in, d_in, q_in,
    out,
    wave, potential, index, values, slot_atom, atom_rank, d_part, q_part, load_sem,
    low_halo, high_halo, turned, row_hot, col_hot, picked, back_rows, acc,
    parts, arrived, windows, send_sem, recv_sem,
):
    bands, planes, ny, nz = wave.shape
    slots, pts = index.shape
    nproj = values.shape[0] // slots
    atoms_dev = d_part.shape[2]
    atoms_all = atom_rank.shape[0]
    ni, ns, si = bands * nproj, bands * slots, slots * nproj
    rows = planes * ny
    wide = bands * nz
    row_shift, lane_mask = log2(nz), nz - 1
    p_bits, s_bits = log2(nproj), log2(slots)

    me = lax.axis_index("dom")

    loads = [
        pltpu.make_async_copy(src, dst, load_sem.at[k])
        for k, (src, dst) in enumerate((
            (wave_in, wave), (index_in, index), (slot_atom_in, slot_atom),
            (atom_rank_in, atom_rank), (values_in, values), (d_in, d_part), (q_in, q_part),
            (potential_in, potential),
        ))
    ]
    for c in loads:
        c.start()

    def device(step):
        return lax.rem(me + step + n_dom, n_dom)

    barrier = pltpu.get_barrier_semaphore()
    for step in STEPS:
        pl.semaphore_signal(barrier, inc=1, device_id={"dom": device(step)}, device_id_type=MESH)

    eye = iota((slots, slots), 0) == iota((slots, slots), 1)
    for c in loads[1:4]:
        c.wait()
    atom = jnp.sum(jnp.where(eye, slot_atom[...].astype(jnp.float32), 0.0), axis=1, keepdims=True)
    rank = atom_rank[...].astype(jnp.float32).reshape(1, atoms_all) + 1.0
    among = iota((slots, atoms_all), 1).astype(jnp.float32) == atom
    position = jnp.sum(jnp.where(among, rank, 0.0), axis=1, keepdims=True)
    place = iota((slots, LANES), 1)
    tables = []
    for b in range(5):
        owned = (place + device(b - 2) * atoms_dev + 1).astype(jnp.float32)
        tables.append(ones_where((owned == position) & (place < atoms_dev)))
    table = jnp.concatenate(tables, axis=1)
    windows[2] = jnp.zeros_like(windows[2])
    acc[...] = jnp.zeros_like(acc)

    loads[0].wait()
    pl.semaphore_wait(barrier, len(STEPS))

    def copy(k, src, dst, step):
        return pltpu.make_async_remote_copy(
            src_ref=src, dst_ref=dst, send_sem=send_sem.at[k], recv_sem=recv_sem.at[k],
            device_id={"dom": device(step)}, device_id_type=MESH,
        )

    halo = [
        copy(0, wave.at[:, planes - 2 : planes], low_halo, 1),
        copy(1, wave.at[:, 0:2], high_halo, -1),
    ]
    for c in halo:
        c.start()

    for n in range(bands):
        high, low = halves(wave[n].reshape(rows, nz).T)
        turned[n * nz : (n + 1) * nz, :] = high
        turned[wide + n * nz : wide + (n + 1) * nz, :] = low

    def gather(group, carry):
        for u in range(unroll):
            s = group * unroll + u
            flat = index[pl.ds(s, 1), :]
            hot = ones_where(
                iota((rows, pts), 0) == lax.shift_right_logical(flat, row_shift)
            ).astype(jnp.bfloat16)
            match = iota((nz, pts), 0) == (flat & lane_mask)
            col_hot[s] = ones_where(match).astype(jnp.bfloat16)
            lines = dot_dims(turned[...], hot, 1, 0)
            for n in range(bands):
                line = lines[n * nz : (n + 1) * nz] + lines[wide + n * nz : wide + (n + 1) * nz]
                line = jnp.where(match, line, 0.0)
                picked[n, pl.ds(s, 1), :] = jnp.sum(line, axis=0, keepdims=True)
        return carry

    lax.fori_loop(0, slots // unroll, gather, 0)

    loads[4].wait()
    same_slot = (iota((ns, si), 0) & (slots - 1)) == lax.shift_right_logical(iota((ns, si), 1), p_bits)
    same_band = lax.shift_right_logical(iota((ns, ni), 0), s_bits) == lax.shift_right_logical(
        iota((ns, ni), 1), p_bits
    )
    spread = ones_where((iota((ni, si), 0) & (nproj - 1)) == (iota((ni, si), 1) & (nproj - 1)))
    pairs = dot_full(picked[...].reshape(ns, pts), values[...], 1, 1)
    pairs = jnp.where(same_slot, pairs, 0.0)
    slot_rows = jnp.where(same_band, dot_hot(pairs, spread, 1, 1), 0.0)
    coeff = jnp.sum(slot_rows.reshape(bands, slots, ni), axis=0)
    partial = dot_hot(coeff.T, table, 1, 0)
    for b in range(5):
        parts[b] = partial[:, b * LANES : (b + 1) * LANES]

    first = [copy(2 + i, parts.at[step + 2], arrived.at[i], step) for i, step in enumerate(STEPS)]
    for c in first:
        c.start()

    by_slot = lax.shift_right_logical(index[...], row_shift).astype(jnp.float32).T
    by_slot = by_slot.astype(jnp.bfloat16)

    def hots(group, carry):
        for u in range(unroll):
            s = group * unroll + u
            chosen = ones_where(iota((slots, rows), 0) == s).astype(jnp.bfloat16)
            spread_rows = dot_dims(by_slot, chosen, 1, 0)
            match = spread_rows == iota((pts, rows), 1).astype(jnp.float32)
            row_hot[s] = ones_where(match).astype(jnp.bfloat16)
        return carry

    def local(some):
        for n in some:
            for x in range(planes):
                f = wave[n, x]
                near, far = jnp.zeros_like(f), jnp.zeros_like(f)
                for axis, size in ((0, ny), (1, nz)):
                    near = near + pltpu.roll(f, 1, axis) + pltpu.roll(f, size - 1, axis)
                    far = far + pltpu.roll(f, 2, axis) + pltpu.roll(f, size - 2, axis)
                for k in (x - 1, x + 1):
                    if 0 <= k < planes:
                        near = near + wave[n, k]
                for k in (x - 2, x + 2):
                    if 0 <= k < planes:
                        far = far + wave[n, k]
                out[n, x] = (
                    (3.75 + potential[x] - energies[n]) * f - (2.0 / 3.0) * near + (1.0 / 24.0) * far
                )

    half = slots // unroll // 2
    lax.fori_loop(0, half, hots, 0)
    loads[7].wait()
    local(range(bands // 2))

    total = parts[2]
    for i, c in enumerate(first):
        c.wait_recv()
        total = total + arrived[i]

    for c in loads[5:7]:
        c.wait()
    for n in range(bands):
        matrix = d_part[...] - energies[n] * q_part[...]
        column = total[n * nproj : (n + 1) * nproj, :atoms_dev]
        windows[2, n * nproj : (n + 1) * nproj, :atoms_dev] = jnp.sum(matrix * column[None], axis=1)

    second = [copy(6 + i, windows.at[2], windows.at[step + 2], -step) for i, step in enumerate(STEPS)]
    for c in second:
        c.start()
    lax.fori_loop(half, slots // unroll, hots, 0)
    local(range(bands // 2, bands))
    for c in second:
        c.wait_recv()

    around = jnp.concatenate([windows[b] for b in range(5)], axis=1)
    slot_weight = dot_hot(around, table, 1, 1).T
    slot_weight = jnp.where(same_band, jnp.concatenate([slot_weight] * bands, axis=0), 0.0)
    blocks = jnp.where(same_slot, dot_hot(slot_weight, spread, 1, 0), 0.0)
    back_rows[...] = dot_full(blocks, values[...], 1, 0).reshape(bands, slots, pts)

    def scatter(group, carry):
        lefts, rights = [], []
        for u in range(unroll):
            s = group * unroll + u
            cols = col_hot[s].reshape(nz // 16, 16, pts)
            high_parts, low_parts = [], []
            for n in range(bands):
                line = jnp.broadcast_to(back_rows[n, pl.ds(s, 1), :], (16, pts))
                high, low = halves(line)
                high_parts.append((cols * high[None]).reshape(nz, pts))
                low_parts.append((cols * low[None]).reshape(nz, pts))
            lefts.append(jnp.concatenate(high_parts + low_parts, axis=0))
            rights.append(row_hot[s])
        acc[...] += dot_dims(jnp.concatenate(lefts, axis=1), jnp.concatenate(rights, axis=0), 1, 0)
        return carry

    lax.fori_loop(0, slots // unroll, scatter, 0)

    for c in halo:
        c.wait_recv()

    def beyond(n, k):
        return low_halo[n, k + 2] if k < 0 else high_halo[n, k - planes]

    for n in range(bands):
        added = acc[n * nz : (n + 1) * nz, :] + acc[wide + n * nz : wide + (n + 1) * nz, :]
        added = added.T.reshape(planes, ny, nz)
        for x in range(planes):
            plane = out[n, x] + added[x]
            for distance, factor in ((1, -2.0 / 3.0), (2, 1.0 / 24.0)):
                for k in (x - distance, x + distance):
                    if not 0 <= k < planes:
                        plane = plane + factor * beyond(n, k)
            out[n, x] = plane

    for c in halo + first + second:
        c.wait_send()


def per_device(
    wave, potential, energies, proj_index, proj_values, slot_atom, atom_rank, d_matrix, q_matrix
):
    bands, planes, ny, nz = wave.shape
    slots, pts = proj_index.shape
    nproj = proj_values.shape[1]
    atoms_dev = d_matrix.shape[0]
    assert atoms_dev <= LANES and nz == LANES
    rows = planes * ny
    f32, bf16 = jnp.float32, jnp.bfloat16
    vmem = pl.BlockSpec(memory_space=pltpu.VMEM)
    atom_block = (bands * nproj, LANES)
    return pl.pallas_call(
        functools.partial(kernel, lax.axis_size("dom"), 16),
        out_shape=jax.ShapeDtypeStruct(wave.shape, f32),
        in_specs=[pl.BlockSpec(memory_space=pltpu.SMEM)]
        + [pl.BlockSpec(memory_space=pltpu.HBM)] * 8,
        out_specs=vmem,
        scratch_shapes=[
            pltpu.VMEM(wave.shape, f32),
            pltpu.VMEM(potential.shape, f32),
            pltpu.VMEM(proj_index.shape, jnp.int32),
            pltpu.VMEM((slots * nproj, pts), f32),
            pltpu.VMEM((1, slots), jnp.int32),
            pltpu.VMEM(atom_rank.shape, jnp.int32),
            pltpu.VMEM((nproj, nproj, atoms_dev), f32),
            pltpu.VMEM((nproj, nproj, atoms_dev), f32),
            pltpu.SemaphoreType.DMA((8,)),
            pltpu.VMEM((bands, 2, ny, nz), f32),
            pltpu.VMEM((bands, 2, ny, nz), f32),
            pltpu.VMEM((2 * bands * nz, rows), bf16),
            pltpu.VMEM((slots, pts, rows), bf16),
            pltpu.VMEM((slots, nz, pts), bf16),
            pltpu.VMEM((bands, slots, pts), f32),
            pltpu.VMEM((bands, slots, pts), f32),
            pltpu.VMEM((2 * bands * nz, rows), f32),
            pltpu.VMEM((5,) + atom_block, f32),
            pltpu.VMEM((4,) + atom_block, f32),
            pltpu.VMEM((5,) + atom_block, f32),
            pltpu.SemaphoreType.DMA((10,)),
            pltpu.SemaphoreType.DMA((10,)),
        ],
        compiler_params=pltpu.CompilerParams(
            collective_id=0, has_side_effects=True, vmem_limit_bytes=60 * 1024 * 1024
        ),
    )(
        energies, wave, potential, proj_index,
        proj_values.reshape(slots * nproj, pts),
        slot_atom.reshape(1, slots), atom_rank,
        jnp.transpose(d_matrix, (1, 2, 0)), jnp.transpose(q_matrix, (1, 2, 0)),
    )


def solution(mesh):
    placed = (
        P("band", "dom", None, None),
        P("dom", None, None),
        P("band"),
        P("dom", None),
        P("dom", None, None),
        P("dom"),
        P(),
        P("dom", None, None),
        P("dom", None, None),
    )
    return jax.shard_map(
        per_device,
        mesh=mesh,
        in_specs=placed,
        out_specs=P("band", "dom", None, None),
        check_vma=False,
    )
```
